32 devices in a mesh: groups: 2 (over x), region: 16 (over z, y, core).
Axes of the slice: x: 2, y: 2, z: 4, core: 2. Of those that a mesh axis runs over, the one named last changes fastest.
Arguments:
- obs_pos: float32 [512, 2, 256], P(('groups', 'region')), parts along dimension 0, may hold values from 0 to 230400, as said below
- obs_sigma: float32 [512, 256], P(('groups', 'region')), parts along dimension 0, may hold values from 0.5 to 1.2
- obs_error: float32 [512, 256], P(('groups', 'region')), parts along dimension 0, may hold values from 0.2 to 2
- innovation: float32 [512, 64, 256], P(('groups', 'region')), parts along dimension 0, may hold values from -6 to 6
- obs_count: int32 [512], P(('groups', 'region')), parts along dimension 0, may hold values from 1 to 256
- pair_list: int32 [2, 3072], P(None, ('groups', 'region')), parts along dimension 1, may hold values from 0 to 255, as said below
- pair_live: int32 [32], P(('groups', 'region')), parts along dimension 0, may hold values from 16 to 96
Outputs:
- solution: float32 [512, 64, 256], P(('groups', 'region')), parts along dimension 0
- residual: float32 [512, 64, 256], P(('groups', 'region')), parts along dimension 0
The draws below stay inside these ranges and needn't reach their ends.
There are 2 independent parts, one for each index of `groups`. The reference program is written for one: setup_inputs(seed, part) draws one part's arguments, and reference() takes and returns one part's arrays. A program takes and returns all parts, laid end to end along the dimension named above; each array names one. Nothing has to cross between parts.
Inputs may be any that keep to these rules, and one draw needn't show every extreme that they name: `obs_pos`: block b's observations lie in cell b, an interval of the first coordinate 300 to 900 km long; cells follow one another without gaps in block order from 0; the second coordinate lies in 0 to 600 km. `pair_list`: device k's 96 slots hold pairs (i, j) with i among its 16 blocks and i <= j <= i + 5; its first pair_live[k] slots list, each once, every pair of such an i with a block j >= i whose cells lie less than 1500 km apart (i = j included); the other slots hold (k * 16, k * 16).
All inputs are finite; a program needn't handle non-finite values.
Results may differ from the reference program's by a relative error of at most 0.0003.
Values sent between devices are 32-bit elements; how exact they have to be, the bound alone decides.
No kernel may reach another device: no remote copies, remote signals or barrier semaphores. Data moves between devices by JAX's collectives and lax.ppermute only.
A program may use at most 64 MiB of HBM per device.

```python
import math
import jax
import jax.numpy as jnp
from jax import lax

BLK = 256
BLOCKS_DEV = 16
MEMBERS = 64
REACH = 5
ITERS = 2
NB = 256
N_REGION = 16


def cell_edges(key):
    key_width, key_crowd = jax.random.split(key)
    widths = jax.random.randint(key_width, (NB,), 300, 901)
    devices = NB // BLOCKS_DEV
    crowded = jax.random.randint(key_crowd, (), 0, max(devices - 1, 1))
    block_ids = jnp.arange(NB, dtype=jnp.int32)
    start_block = crowded * BLOCKS_DEV
    inside = (block_ids >= start_block) & (block_ids < start_block + BLOCKS_DEV + REACH)
    widths = jnp.where(inside, 300, widths).astype(jnp.int32)
    lefts = (jnp.cumsum(widths) - widths).astype(jnp.int32)
    return (widths, lefts)


def pair_table(key):
    widths, lefts = cell_edges(key)
    rights = lefts + widths
    devices = NB // BLOCKS_DEV
    slot_count = BLOCKS_DEV * (REACH + 1)
    block_ids = jnp.arange(NB, dtype=jnp.int32)[:, None]
    offsets = jnp.arange(REACH + 1, dtype=jnp.int32)[None, :]
    partner = block_ids + offsets
    clipped = jnp.minimum(partner, NB - 1)
    linked = (partner < NB) & ((offsets == 0) | (lefts[clipped] - rights[:, None] < 1500))
    linked = linked.reshape(devices, slot_count)
    owners = jnp.broadcast_to(block_ids, (NB, REACH + 1)).reshape(devices, slot_count)
    partners = clipped.reshape(devices, slot_count)
    slot_ids = jnp.arange(slot_count, dtype=jnp.int32)[None, :]
    scores = jnp.where(linked, 0, slot_count) + slot_ids
    ordering = jnp.argsort(scores, axis=1)
    counts = jnp.sum(linked.astype(jnp.int32), axis=1)
    filled = slot_ids < counts[:, None]
    base_block = (jnp.arange(devices, dtype=jnp.int32) * BLOCKS_DEV)[:, None]
    firsts = jnp.where(filled, jnp.take_along_axis(owners, ordering, axis=1), base_block)
    seconds = jnp.where(filled, jnp.take_along_axis(partners, ordering, axis=1), base_block)
    listing = jnp.stack([firsts.reshape(-1), seconds.reshape(-1)]).astype(jnp.int32)
    return (listing, counts.astype(jnp.int32))


def draw_pair_list(key, part):
    listing, counts = pair_table(key)
    return listing


def draw_pair_live(key, part):
    listing, counts = pair_table(key)
    return counts


def draw_obs_count(key, part):
    key = jax.random.fold_in(key, 5)
    key_count, key_full = jax.random.split(key)
    counts = jax.random.randint(key_count, (NB,), 1, BLK + 1)
    chosen = jax.random.randint(key_full, (), 0, NB)
    return jnp.where(jnp.arange(NB, dtype=jnp.int32) == chosen, BLK, counts).astype(jnp.int32)


def draw_obs_pos(key, part):
    widths, lefts = cell_edges(key)
    key = jax.random.fold_in(key, 3)
    key_along, key_across = jax.random.split(key)
    along = jax.random.uniform(key_along, (NB, BLK), jnp.float32)
    across = jax.random.uniform(key_across, (NB, BLK), jnp.float32)
    coord_x = lefts.astype(jnp.float32)[:, None] + along * widths.astype(jnp.float32)[:, None]
    coord_y = across * 600.0
    return jnp.stack([coord_x, coord_y], axis=1).astype(jnp.float32)


def block_scale(stream_key, extent, cuts, least, high):
    level = 1.0
    for dim, blocks in cuts:
        steps = jax.random.uniform(jax.random.fold_in(jax.random.fold_in(stream_key, 6), dim), (blocks,), jnp.float32, least / len(cuts), high / len(cuts))
        level = level * jnp.repeat(jnp.exp(steps), extent[dim] // blocks).reshape((-1,) + (1,) * (len(extent) - 1 - dim))
    return level


def centred(own_key, dims, spread, limit, shards=(), held_as=jnp.bfloat16):
    drawn = spread * jax.random.normal(own_key, dims, jnp.float32)
    if shards:
        drawn = drawn * block_scale(own_key, dims, shards, -0.22, 0.18)
    return jnp.clip(drawn, -limit, limit).astype(held_as)


def setup_inputs(seed: int = 0, part: int = 0) -> dict:
    key_list = jax.random.split(jax.random.key(seed), 8)
    part_keys = jax.random.split(jax.random.fold_in(key_list[7], part), 8)
    obs_pos = draw_obs_pos(jax.random.fold_in(jax.random.fold_in(key_list[7], part), 71), part)
    obs_sigma = jnp.clip(jnp.exp(math.log(1.2) - 0.8754688 * jax.random.uniform(part_keys[1], (NB, BLK), jnp.float32) ** block_scale(part_keys[1], (NB, BLK), ((0, 16),), -0.2, 0.2)), 0.5, 1.2)
    obs_error = jnp.clip(jnp.exp(math.log(2.0) - 2.3025851 * jax.random.uniform(part_keys[2], (NB, BLK), jnp.float32) ** block_scale(part_keys[2], (NB, BLK), ((0, 16),), -0.2, 0.2)), 0.2, 2.0)
    innovation = centred(part_keys[3], (NB, MEMBERS, BLK), 1.0, 6.0, ((0, 16),), jnp.float32)
    obs_count = draw_obs_count(jax.random.fold_in(jax.random.fold_in(key_list[7], part), 71), part)
    pair_list = draw_pair_list(jax.random.fold_in(jax.random.fold_in(key_list[7], part), 71), part)
    pair_live = draw_pair_live(jax.random.fold_in(jax.random.fold_in(key_list[7], part), 71), part)
    return dict(obs_pos=obs_pos, obs_sigma=obs_sigma, obs_error=obs_error, innovation=innovation, obs_count=obs_count, pair_list=pair_list, pair_live=pair_live)


CUTOFF_KM = 1500.0
SCALE_KM = 1000.0

def build_tiles(geo_first, geo_second):
    delta_x = geo_first[:, 0, :, None] - geo_second[:, 0, None, :]
    delta_y = geo_first[:, 1, :, None] - geo_second[:, 1, None, :]
    distance = jnp.sqrt(delta_x * delta_x + delta_y * delta_y)
    tapered = jnp.maximum(1.0 - distance / CUTOFF_KM, 0.0)
    return geo_first[:, 2, :, None] * geo_second[:, 2, None, :] * (jnp.exp(-distance / SCALE_KM) * tapered * tapered)

def reference(obs_pos, obs_sigma, obs_error, innovation, obs_count, pair_list, pair_live):
    obs_mask = (jnp.arange(BLK, dtype=jnp.int32)[None, :] < obs_count[:, None]).astype(jnp.float32)
    geometry = jnp.concatenate([obs_pos, (obs_sigma * obs_mask)[:, None, :]], axis=1)
    slot_count = pair_list.shape[1] // N_REGION

    def operate(direction):

        def per_device(totals, device):
            first_idx = lax.dynamic_slice_in_dim(pair_list[0], device * slot_count, slot_count)
            second_idx = lax.dynamic_slice_in_dim(pair_list[1], device * slot_count, slot_count)
            is_live = jnp.arange(slot_count, dtype=jnp.int32) < pair_live[device]
            tiles = build_tiles(geometry[first_idx], geometry[second_idx])
            forward_terms = jnp.einsum('pab,pmb->pma', tiles, direction[second_idx], precision=lax.Precision.HIGHEST)
            transposed = jnp.einsum('pab,pma->pmb', tiles, direction[first_idx], precision=lax.Precision.HIGHEST)
            forward_weight = is_live.astype(jnp.float32)[:, None, None]
            transposed_weight = (is_live & (first_idx != second_idx)).astype(jnp.float32)[:, None, None]
            totals = totals.at[first_idx].add(forward_terms * forward_weight)
            totals = totals.at[second_idx].add(transposed * transposed_weight)
            return (totals, None)
        totals, ignored = lax.scan(per_device, jnp.zeros_like(direction), jnp.arange(N_REGION, dtype=jnp.int32))
        return totals + obs_error[:, None, :] * direction
    residual = innovation * obs_mask[:, None, :]
    solution = jnp.zeros_like(residual)
    direction = residual
    norm_now = lax.optimization_barrier(jnp.sum(residual * residual, axis=(0, 2)))
    for iteration in range(ITERS):
        image = operate(direction)
        alpha = norm_now / lax.optimization_barrier(jnp.sum(direction * image, axis=(0, 2)))
        solution = solution + alpha[None, :, None] * direction
        residual = residual - alpha[None, :, None] * image
        norm_next = lax.optimization_barrier(jnp.sum(residual * residual, axis=(0, 2)))
        direction = residual + (norm_next / norm_now)[None, :, None] * direction
        norm_now = norm_next
    return (solution, residual)
```

```python
import functools

import jax
import jax.numpy as jnp
from jax import lax
from jax.experimental import pallas as pl
from jax.experimental.pallas import tpu as pltpu
from jax.sharding import PartitionSpec as P

REACH = 5
CUTOFF_KM = 1500.0
SCALE_KM = 1000.0
LOG2E = 1.4426950408889634
UNIT = LOG2E / SCALE_KM
TAPER = 1.0 / (CUTOFF_KM * UNIT)
LIMIT = CUTOFF_KM * UNIT
CH = 256
LN = 128
SPAN = 7
TINY = 1e-30
F32, BF16, I32 = jnp.float32, jnp.bfloat16, jnp.int32
VM = pl.BlockSpec(memory_space=pltpu.VMEM)
SM = pl.BlockSpec(memory_space=pltpu.SMEM)
HB = pl.BlockSpec(memory_space=pltpu.HBM)
MB = 1 << 20


def lanes(shape):
    return lax.broadcasted_iota(I32, shape, len(shape) - 1)


def at(start, size=CH):
    return pl.ds(pl.multiple_of(start, LN), size)


def pack_block(rows, count, offset, dst):
    base = (offset // LN) * LN
    shift = offset - base
    lane = lanes((rows.shape[0], LN))
    low = pltpu.roll(jnp.where(lane < count, rows[:, :LN], 0.0), shift, 1)
    high = pltpu.roll(jnp.where(lane + LN < count, rows[:, LN:], 0.0), shift, 1)
    before = lane < shift
    dst[:, at(base, LN)] = jnp.where(before, dst[:, at(base, LN)], low)
    dst[:, at(base + LN, LN)] = jnp.where(before, low, high)
    dst[:, at(base + 2 * LN, LN)] = jnp.where(before, high, 0.0)
    dst[:, at(base + 3 * LN, LN)] = jnp.zeros_like(low)


def split(values):
    high = values.astype(BF16)
    return high, (values - high.astype(F32)).astype(BF16)


def put_split(values, dst, place):
    high, low = split(values)
    half = values.shape[0]
    dst[place, :half, :] = high
    dst[place, half:, :] = low


def columns(row):
    parts = [jnp.broadcast_to(row[:, k : k + LN], (LN, LN)).T for k in (0, LN)]
    return jnp.concatenate(parts, axis=0)


def build(col_x, col_y, place, row_x, row_y, tile_ref, slot):
    strip = 32
    for top in range(0, CH, strip):
        for left in range(0, CH, LN):
            dx = col_x[place, top : top + strip, :] - row_x[:, left : left + LN]
            dy = col_y[place, top : top + strip, :] - row_y[:, left : left + LN]
            square = jnp.maximum(dx * dx + dy * dy, TINY)
            distance = square * lax.rsqrt(square)
            tapered = jnp.maximum(1.0 - distance * TAPER, 0.0)
            value = jnp.exp2(-distance) * (tapered * tapered)
            high, low = split(value)
            tile_ref[slot, top : top + strip, left : left + LN] = high
            tile_ref[slot, CH + top : CH + top + strip, left : left + LN] = low


def product(parts_ref, place, tile_ref, slot, transposed):
    dims = (((1,), (1 if transposed else 0,)), ((), ()))
    both = parts_ref[place]
    half = both.shape[0] // 2
    wide = lax.dot_general(both, tile_ref[slot, :CH, :], dims, preferred_element_type=F32)
    fine = lax.dot_general(both[:half], tile_ref[slot, CH:, :], dims, preferred_element_type=F32)
    return wide[:half] + wide[half:] + fine


def own_product(t, total, down, across, parts_ref, tile_ref, slot, acc):
    i, j = down[t], across[t]
    here = (t < total).astype(F32)
    other = jnp.where((t < total) & (i != j), 1.0, 0.0).astype(F32)
    forward = product(parts_ref, i, tile_ref, slot, False)
    backward = product(parts_ref, j, tile_ref, slot, True)
    acc[:, at(j * CH)] += here * forward
    acc[:, at(i * CH)] += other * backward


def edge_product(t, total, down, across, parts_ref, tile_ref, slot, acc):
    here = (t < total).astype(F32)
    acc[:, at(across[t] * CH)] += here * product(parts_ref, down[t], tile_ref, slot, False)


def fetch(pairs, sems):
    copies = [pltpu.make_async_copy(src, dst, sems.at[k]) for k, (src, dst) in enumerate(pairs)]
    for copy in copies:
        copy.start()
    for copy in copies:
        copy.wait()


def pack_sides(innov, pos_in, sigma_in, count_in, to_prev, to_next, pos, sigma, count, sems):
    blocks, members = innov.shape[0], innov.shape[1]
    ends = ((0, to_prev), (blocks - REACH, to_next))
    pairs = [(pos_in, pos), (sigma_in, sigma), (count_in, count)]
    for first, dst in ends:
        pairs.append((innov.at[pl.ds(first, REACH)], dst.at[:, pl.ds(0, members), :]))
    fetch(pairs, sems)
    for first, dst in ends:
        for b in range(REACH):
            number = jnp.full((1, CH), count[first + b].astype(F32))
            rest = jnp.zeros((4, CH), F32)
            dst[b, members:, :] = jnp.concatenate(
                [pos[first + b], sigma[first + b : first + b + 1, :], number, rest], axis=0
            )


def own_kernel(innov_in, pos_in, sigma_in, err_in, count_in, ev, od, vec, geo, acc, ints, floats,
               down, across, innov, pos, sigma, err, count, parts, col_x, col_y, sems):
    blocks = innov.shape[0]
    fetch(
        [(innov_in, innov), (pos_in, pos), (sigma_in, sigma), (err_in, err), (count_in, count)],
        sems,
    )
    acc[...] = jnp.zeros_like(acc)
    origin = pos[0, 0:1, 0:1]

    def pack(b, offset):
        number = count[b]
        ints[b] = offset
        pack_block(innov[b], number, offset, vec)
        pair = pos[b]
        rows = jnp.concatenate(
            [
                (pair[0:1] - origin) * UNIT,
                pair[1:2] * UNIT,
                sigma[pl.ds(b, 1), :],
                err[pl.ds(b, 1), :],
                jnp.zeros((4, CH), F32),
            ],
            axis=0,
        )
        pack_block(rows, number, offset, geo)
        return offset + number

    size = lax.fori_loop(0, blocks, pack, jnp.int32(0))
    ints[blocks] = size
    chunks = (size + CH - 1) // CH
    floats[0] = jnp.max(origin)

    def prepare(i, carry):
        where = at(i * CH)
        x = geo[0:1, where]
        col_x[i] = columns(x)
        col_y[i] = columns(geo[1:2, where])
        put_split(vec[:, where] * geo[2:3, where], parts, i)
        live = lanes((1, CH)) + i * CH < size
        floats[1 + i] = jnp.min(jnp.where(live, x, 3e38))
        floats[1 + blocks + i] = jnp.max(jnp.where(live, x, -3e38))
        return carry

    lax.fori_loop(0, chunks, prepare, 0)

    def enlist(i, t):
        end = floats[1 + blocks + i]
        for d in range(SPAN):
            j = i + d
            start = floats[1 + jnp.minimum(j, blocks - 1)]
            down[t] = i
            across[t] = j
            t = t + jnp.where((j < chunks) & (start - end < LIMIT), 1, 0)
        return t

    total = lax.fori_loop(0, chunks, enlist, jnp.int32(0))
    for extra in range(3):
        down[total + extra] = 0
        across[total + extra] = 0
    ints[blocks + 1] = total

    def make(t, ref, slot):
        where = at(across[t] * CH)
        build(col_x, col_y, down[t], geo[0:1, where], geo[1:2, where], ref, slot)

    make(0, ev, 0)

    def step(p, carry):
        t = 2 * p
        make(t + 1, od, p)
        own_product(t, total, down, across, parts, ev, p, acc)
        make(t + 2, ev, p + 1)
        own_product(t + 1, total, down, across, parts, od, p, acc)
        return carry

    lax.fori_loop(0, (total + 1) // 2, step, 0)


def edge_kernel(behind, ahead, vec, geo, acc, ints, floats, ev, od, side_geo, side_ints, down,
                across, out, parts, to_prev, to_next, side_vec, side_parts, col_x, col_y):
    members = vec.shape[0]
    blocks = (vec.shape[1] - 2 * CH) // CH
    wide = side_vec.shape[1] // 2
    size = ints[blocks]
    chunks = (size + CH - 1) // CH
    origin = floats[0]
    out[...] = jnp.zeros_like(out)
    side_ends = []
    for side, ref in enumerate((behind, ahead)):
        offset = jnp.int32(side * wide)
        for b in range(REACH):
            misc = ref[b, members:, :]
            number = misc[3, 0].astype(I32)
            pack_block(ref[b, :members, :], number, offset, side_vec)
            rows = jnp.concatenate(
                [(misc[0:1] - origin) * UNIT, misc[1:2] * UNIT, misc[2:]], axis=0
            )
            pack_block(rows, number, offset, side_geo)
            offset = offset + number
        side_ends.append(offset)
    total = jnp.int32(0)
    down[0] = 0
    across[0] = 0
    for side, end in enumerate(side_ends):
        begin = side * (wide // CH)
        side_chunks = (end - side * wide + CH - 1) // CH

        def prepare(h, t, begin=begin, end=end, side=side):
            place = begin + h
            where = at(place * CH)
            x = side_geo[0:1, where]
            col_x[place] = columns(x)
            col_y[place] = columns(side_geo[1:2, where])
            put_split(side_vec[:, where] * side_geo[2:3, where], side_parts, place)
            live = lanes((1, CH)) + place * CH < end
            if side == 0:
                edge = jnp.max(jnp.where(live, x, -3e38))
            else:
                edge = jnp.min(jnp.where(live, x, 3e38))
            for d in range(SPAN):
                if side == 0:
                    i = jnp.minimum(d, chunks - 1)
                    near = floats[1 + i] - edge < LIMIT
                else:
                    i = jnp.maximum(chunks - 1 - d, 0)
                    near = edge - floats[1 + blocks + i] < LIMIT
                down[t] = place
                across[t] = i
                t = t + jnp.where(near & (d < chunks), 1, 0)
            return t

        total = lax.fori_loop(0, side_chunks, prepare, total)
    last = jnp.maximum(total - 1, 0)
    for extra in range(3):
        down[total + extra] = down[last]
        across[total + extra] = across[last]
    side_ints[0] = total

    def make(t, ref, slot):
        where = at(across[t] * CH)
        build(col_x, col_y, down[t], geo[0:1, where], geo[1:2, where], ref, slot)

    make(0, ev, 0)

    def step(p, carry):
        t = 2 * p
        make(t + 1, od, p)
        edge_product(t, total, down, across, side_parts, ev, p, out)
        make(t + 2, ev, p + 1)
        edge_product(t + 1, total, down, across, side_parts, od, p, out)
        return carry

    lax.fori_loop(0, (total + 1) // 2, step, 0)

    def finish(i, carry):
        where = at(i * CH)
        scale = geo[2:3, where]
        image = scale * (out[:, where] + acc[:, where]) + geo[3:4, where] * vec[:, where]
        out[:, where] = image
        put_split(image * scale, parts, i)
        return carry

    lax.fori_loop(0, chunks, finish, 0)
    to_prev[...] = out[:, : REACH * CH]
    start = ints[blocks - REACH]
    base = (start // LN) * LN
    shift = start - base
    back = lax.rem(LN - shift, LN)
    keep = lanes((members, LN)) < LN - shift
    turned = pltpu.roll(out[:, at(base, LN)], back, 1)
    for k in range(REACH * CH // LN):
        following = pltpu.roll(out[:, at(base + (k + 1) * LN, LN)], back, 1)
        to_next[:, k * LN : (k + 1) * LN] = jnp.where(keep, turned, following)
        turned = following


def again_kernel(ev, od, parts, ints, down, across, acc):
    blocks = acc.shape[1] // CH - 2
    total = ints[blocks + 1]
    acc[...] = jnp.zeros_like(acc)

    def step(p, carry):
        t = 2 * p
        own_product(t, total, down, across, parts, ev, p, acc)
        own_product(t + 1, total, down, across, parts, od, p, acc)
        return carry

    lax.fori_loop(0, (total + 1) // 2, step, 0)


def lane_sum(values):
    return jnp.sum(values, axis=1, keepdims=True)


def last_kernel(behind, ahead, side_geo, side_ints, ev, od, down, across, acc, vec, image, geo,
                ints, out, sums, side_parts, total_ref):
    members = vec.shape[0]
    blocks = vec.shape[1] // CH - 2
    chunks = (ints[blocks] + CH - 1) // CH
    total = side_ints[0]
    total_ref[...] = acc[...]
    per_side = side_geo.shape[1] // CH // 2
    for side, ref in enumerate((behind, ahead)):
        for h in range(REACH):
            place = side * per_side + h
            scale = side_geo[2:3, place * CH : (place + 1) * CH]
            scaled = jnp.where(scale > 0, ref[:, h * CH : (h + 1) * CH] * scale, 0.0)
            put_split(scaled, side_parts, place)

    def step(p, carry):
        t = 2 * p
        edge_product(t, total, down, across, side_parts, ev, p, total_ref)
        edge_product(t + 1, total, down, across, side_parts, od, p, total_ref)
        return carry

    lax.fori_loop(0, (total + 1) // 2, step, 0)
    out[...] = jnp.zeros_like(out)
    zero = jnp.zeros((members, 1), F32)

    def first(i, carry):
        m0, m1 = carry
        where = at(i * CH)
        r, y = vec[:, where], image[:, where]
        out[:, where] = geo[2:3, where] * total_ref[:, where] + geo[3:4, where] * y
        return m0 + lane_sum(r * r), m1 + lane_sum(r * y)

    m0, m1 = lax.fori_loop(0, chunks, first, (zero, zero))
    mean = jnp.where(m0 > 0, m1 / jnp.where(m0 > 0, m0, 1.0), 0.0)

    def second(i, carry):
        vv, zu, cross, slip = carry
        where = at(i * CH)
        r, y = vec[:, where], image[:, where]
        z = y - mean * r
        u = out[:, where] - mean * y
        return (
            vv + lane_sum(z * z),
            zu + lane_sum(z * u),
            cross + lane_sum(z * y + r * u),
            slip + lane_sum(z * r),
        )

    found = lax.fori_loop(0, chunks, second, (zero, zero, zero, zero))
    table = jnp.zeros((members, LN), F32)
    lane = lanes((members, LN))
    for k, value in enumerate((m0, m1, mean) + tuple(found)):
        table = jnp.where(lane == k, value, table)
    turned = jnp.concatenate([table, jnp.zeros((LN - members, LN), F32)], axis=0).T[:8]
    for k in range(sums.shape[0]):
        sums[k] = turned


def update_kernel(sums, vec, image, second, ints, count, solution_ref, residual_ref, packed):
    members = vec.shape[0]
    blocks = vec.shape[1] // CH - 2
    chunks = (ints[blocks] + CH - 1) // CH
    terms = sums[...]
    m0 = jnp.sum(terms[:, 0, :], axis=0, keepdims=True)
    m1 = jnp.sum(terms[:, 1, :], axis=0, keepdims=True)
    used = lanes((1, LN)) < members
    m0 = jnp.where(used, m0, 1.0)
    m1 = jnp.where(used, m1, 1.0)
    mean = m1 / m0
    off = mean - terms[:, 2, :]
    vv = terms[:, 3, :] - 2.0 * off * terms[:, 6, :] + off * off * terms[:, 0, :]
    zu = terms[:, 4, :] - off * terms[:, 5, :] + off * off * terms[:, 1, :]
    cross = terms[:, 5, :] - 2.0 * off * terms[:, 1, :]
    vv, zu, cross = (jnp.sum(x, axis=0, keepdims=True) for x in (vv, zu, cross))
    alpha = m0 / m1
    rr = alpha * alpha * vv
    beta = rr / m0
    alpha_next = rr / (alpha * alpha * zu - alpha * beta * cross + beta * beta * m1)
    one = alpha + alpha_next * (1.0 + beta)
    two = alpha * alpha_next
    table = jnp.concatenate([one, two, jnp.zeros((LN - 2, LN), F32)], axis=0).T
    one, two = table[:members, 0:1], table[:members, 1:2]

    packed[...] = jnp.zeros_like(packed)

    def combine(i, carry):
        where = at(i * CH)
        r, y, yy = vec[:, where], image[:, where], second[:, where]
        packed[:members, where] = one * r - two * y
        packed[members:, where] = r - one * y + two * yy
        return carry

    lax.fori_loop(0, chunks, combine, 0)

    def unpack(b, carry):
        offset, number = ints[b], count[b]
        base = (offset // LN) * LN
        shift = offset - base
        back = lax.rem(LN - shift, LN)
        lane = lanes((2 * members, LN))
        keep = lane < LN - shift
        turned = [pltpu.roll(packed[:, at(base + k * LN, LN)], back, 1) for k in range(3)]
        for k in range(2):
            part = jnp.where(keep, turned[k], turned[k + 1])
            part = jnp.where(lane + k * LN < number, part, 0.0)
            solution_ref[b, :, k * LN : (k + 1) * LN] = part[:members]
            residual_ref[b, :, k * LN : (k + 1) * LN] = part[members:]
        return carry

    lax.fori_loop(0, blocks, unpack, 0)


def shift_by(block, distance):
    devices = range(lax.axis_size("region"))
    route = [(i, i + distance) for i in devices if i + distance in devices]
    return lax.ppermute(block, "region", route)


def call(kernel, name, in_specs, outs, scratch=(), limit=9 * MB, cost=None):
    return pl.pallas_call(
        kernel,
        name=name,
        in_specs=in_specs,
        out_specs=[spec for spec, _ in outs],
        out_shape=[shape for _, shape in outs],
        scratch_shapes=list(scratch),
        compiler_params=pltpu.CompilerParams(vmem_limit_bytes=limit),
        cost_estimate=cost,
    )


def body(obs_pos, obs_sigma, obs_error, innovation, obs_count, pair_list, pair_live):
    blocks, members, _ = innovation.shape
    sd = jax.ShapeDtypeStruct
    in_hbm = functools.partial(pltpu.with_memory_space_constraint, memory_space=pltpu.HBM)
    in_vmem = functools.partial(pltpu.with_memory_space_constraint, memory_space=pltpu.VMEM)
    wide = blocks * CH + 2 * CH
    side_chunks = REACH + 2
    own_tiles = (blocks * SPAN - SPAN * (SPAN - 1) // 2) // 2 + 3
    side_tiles = 2 * 25 // 2 + 3
    listed = 2 * own_tiles + 16
    pack_out = (VM, sd((REACH, members + 8, CH), F32))
    to_prev, to_next = call(
        pack_sides, "pack", [HB] * 4, [pack_out, pack_out],
        [
            pltpu.VMEM(obs_pos.shape, F32),
            pltpu.VMEM(obs_sigma.shape, F32),
            pltpu.SMEM(obs_count.shape, I32),
            pltpu.SemaphoreType.DMA((5,)),
        ],
        limit=3 * MB,
    )(*map(in_hbm, (innovation, obs_pos, obs_sigma, obs_count)))
    ahead = shift_by(to_prev, -1)
    behind = shift_by(to_next, 1)
    dense = (VM, sd((members, wide), F32))
    tile = (2 * CH, CH)
    ev, od, vec, geo, acc, ints, floats, down, across = call(
        own_kernel, "own", [HB] * 5,
        [
            (VM, pltpu.VMEM((own_tiles,) + tile, BF16)),
            (VM, pltpu.VMEM((own_tiles,) + tile, BF16)),
            dense,
            (VM, sd((8, wide), F32)),
            dense,
            (SM, sd((blocks + 2,), I32)),
            (SM, sd((2 * blocks + 1,), F32)),
            (SM, sd((listed,), I32)),
            (SM, sd((listed,), I32)),
        ],
        [
            pltpu.VMEM(innovation.shape, F32),
            pltpu.VMEM(obs_pos.shape, F32),
            pltpu.VMEM(obs_sigma.shape, F32),
            pltpu.VMEM(obs_error.shape, F32),
            pltpu.SMEM(obs_count.shape, I32),
            pltpu.VMEM((blocks, 2 * members, CH), BF16),
            pltpu.VMEM((blocks, CH, LN), F32),
            pltpu.VMEM((blocks, CH, LN), F32),
            pltpu.SemaphoreType.DMA((5,)),
        ],
        cost=pl.CostEstimate(flops=4 * 10**9, bytes_accessed=20 * MB, transcendentals=0),
    )(*map(in_hbm, (innovation, obs_pos, obs_sigma, obs_error, obs_count)))
    ev, od = in_vmem(ev), in_vmem(od)
    side = (VM, sd((members, REACH * CH), F32))
    (side_ev, side_od, side_geo, side_ints, side_down, side_across, image, parts, image_prev,
     image_next) = call(
        edge_kernel, "edge", [VM, VM, VM, VM, VM, SM, SM],
        [
            (VM, pltpu.VMEM((side_tiles,) + tile, BF16)),
            (VM, pltpu.VMEM((side_tiles,) + tile, BF16)),
            (VM, sd((8, 2 * side_chunks * CH), F32)),
            (SM, sd((1,), I32)),
            (SM, sd((128,), I32)),
            (SM, sd((128,), I32)),
            dense,
            (VM, sd((blocks, 2 * members, CH), BF16)),
            side,
            side,
        ],
        [
            pltpu.VMEM((members, 2 * side_chunks * CH), F32),
            pltpu.VMEM((2 * side_chunks, 2 * members, CH), BF16),
            pltpu.VMEM((2 * side_chunks, CH, LN), F32),
            pltpu.VMEM((2 * side_chunks, CH, LN), F32),
        ],
        limit=7 * MB,
    )(behind, ahead, vec, geo, acc, ints, floats)
    side_ev, side_od = in_vmem(side_ev), in_vmem(side_od)
    image_ahead = shift_by(image_prev, -1)
    image_behind = shift_by(image_next, 1)
    (acc,) = call(
        again_kernel, "again", [VM, VM, VM, SM, SM, SM], [dense], limit=2 * MB,
        cost=pl.CostEstimate(flops=4 * 10**9, bytes_accessed=20 * MB, transcendentals=0),
    )(ev, od, parts, ints, down, across)
    devices = lax.axis_size("region")
    second, sums = call(
        last_kernel, "last", [VM, VM, VM, SM, VM, VM, SM, SM, VM, VM, VM, VM, SM],
        [dense, (VM, sd((devices, 8, LN), F32))],
        [
            pltpu.VMEM((2 * side_chunks, 2 * members, CH), BF16),
            pltpu.VMEM((members, wide), F32),
        ],
        limit=4 * MB,
    )(image_behind, image_ahead, side_geo, side_ints, side_ev, side_od, side_down, side_across,
      acc, vec, image, geo, ints)
    sums = lax.all_to_all(sums, "region", 0, 0)
    field = (VM, sd((blocks, members, CH), F32))
    return tuple(call(
        update_kernel, "update", [VM, VM, VM, VM, SM, SM], [field, field],
        [pltpu.VMEM((2 * members, wide), F32)],
        limit=6 * MB,
    )(sums, vec, image, second, ints, obs_count))


def solution(mesh):
    return jax.shard_map(
        body,
        mesh=mesh,
        in_specs=(
            P(("groups", "region"), None, None),
            P(("groups", "region"), None),
            P(("groups", "region"), None),
            P(("groups", "region"), None, None),
            P(("groups", "region")),
            P(None, ("groups", "region")),
            P(("groups", "region")),
        ),
        out_specs=(P(("groups", "region"), None, None), P(("groups", "region"), None, None)),
        check_vma=False,
    )
```

```python
import functools

import jax
import jax.numpy as jnp
from jax import lax
from jax.experimental import pallas as pl
from jax.experimental.pallas import tpu as pltpu
from jax.sharding import PartitionSpec as P

REACH = 5
CUTOFF_KM = 1500.0
SCALE_KM = 1000.0
LOG2E = 1.4426950408889634
UNIT = LOG2E / SCALE_KM
TAPER = 1.0 / (CUTOFF_KM * UNIT)
LIMIT = CUTOFF_KM * UNIT
CH = 256
LN = 128
BATCH = 8
SPAN = 7
TINY = 1e-30
F32, BF16, I32 = jnp.float32, jnp.bfloat16, jnp.int32
VM = pl.BlockSpec(memory_space=pltpu.VMEM)
SM = pl.BlockSpec(memory_space=pltpu.SMEM)
HB = pl.BlockSpec(memory_space=pltpu.HBM)
MB = 1 << 20
OWN_HELD = 64
SIDE_HELD = 24


def lanes(shape):
    return lax.broadcasted_iota(I32, shape, len(shape) - 1)


def at(start, size=CH):
    return pl.ds(pl.multiple_of(start, LN), size)


def pack_block(rows, count, offset, dst):
    base = (offset // LN) * LN
    shift = offset - base
    lane = lanes((rows.shape[0], LN))
    low = pltpu.roll(jnp.where(lane < count, rows[:, :LN], 0.0), shift, 1)
    high = pltpu.roll(jnp.where(lane + LN < count, rows[:, LN:], 0.0), shift, 1)
    before = lane < shift
    dst[:, at(base, LN)] = jnp.where(before, dst[:, at(base, LN)], low)
    dst[:, at(base + LN, LN)] = jnp.where(before, low, high)
    dst[:, at(base + 2 * LN, LN)] = jnp.where(before, high, 0.0)
    dst[:, at(base + 3 * LN, LN)] = jnp.zeros_like(low)


def split(values):
    high = values.astype(BF16)
    return high, (values - high.astype(F32)).astype(BF16)


def put_split(values, dst, place):
    high, low = split(values)
    half = values.shape[0]
    dst[place, :half, :] = high
    dst[place, half:, :] = low


def columns(row):
    parts = [jnp.broadcast_to(row[:, k : k + LN], (LN, LN)).T for k in (0, LN)]
    return jnp.concatenate(parts, axis=0)


def build(col_x, col_y, place, row_x, row_y, tile_ref, slot):
    strip = 32
    for top in range(0, CH, strip):
        for left in range(0, CH, LN):
            dx = col_x[place, top : top + strip, :] - row_x[:, left : left + LN]
            dy = col_y[place, top : top + strip, :] - row_y[:, left : left + LN]
            square = jnp.maximum(dx * dx + dy * dy, TINY)
            distance = square * lax.rsqrt(square)
            tapered = jnp.maximum(1.0 - distance * TAPER, 0.0)
            value = jnp.exp2(-distance) * (tapered * tapered)
            high, low = split(value)
            tile_ref[slot, top : top + strip, left : left + LN] = high
            tile_ref[slot, CH + top : CH + top + strip, left : left + LN] = low


def product(parts_ref, place, tile_ref, slot, transposed):
    dims = (((1,), (1 if transposed else 0,)), ((), ()))
    both = parts_ref[place]
    half = both.shape[0] // 2
    wide = lax.dot_general(both, tile_ref[slot, :CH, :], dims, preferred_element_type=F32)
    fine = lax.dot_general(both[:half], tile_ref[slot, CH:, :], dims, preferred_element_type=F32)
    return wide[:half] + wide[half:] + fine


def own_product(t, total, down, across, parts_ref, tile_ref, slot, acc):
    i, j = down[t], across[t]
    here = (t < total).astype(F32)
    other = jnp.where((t < total) & (i != j), 1.0, 0.0).astype(F32)
    forward = product(parts_ref, i, tile_ref, slot, False)
    backward = product(parts_ref, j, tile_ref, slot, True)
    acc[:, at(j * CH)] += here * forward
    acc[:, at(i * CH)] += other * backward


def edge_product(t, total, down, across, parts_ref, tile_ref, slot, acc):
    here = (t < total).astype(F32)
    acc[:, at(across[t] * CH)] += here * product(parts_ref, down[t], tile_ref, slot, False)


def sweep(total, held, make, multiply):
    pairs = (total + 1) // 2
    full = jnp.minimum(total, 2 * held) // BATCH

    def many(p, carry):
        for half in (make, multiply):
            for u in range(BATCH):
                if half is not None:
                    half(BATCH * p + u, u % 2, BATCH // 2 * p + u // 2)
        return carry

    def few(p, carry):
        for half in (make, multiply):
            for u in range(2):
                if half is not None:
                    half(2 * p + u, u, jnp.minimum(p, held))
        return carry

    lax.fori_loop(0, full, many, 0)
    end = pairs if make is not None else jnp.minimum(pairs, held)
    lax.fori_loop(full * (BATCH // 2), end, few, 0)


def sweep_rest(total, held, make, multiply):
    def few(p, carry):
        for half in (make, multiply):
            for u in range(2):
                half(2 * p + u, u, 0)
        return carry

    lax.fori_loop(held, (total + 1) // 2, few, 0)


def remake(t, down, across, down_geo, geo, col_x, col_y, ref):
    where = at(down[t] * CH)
    col_x[0] = columns(down_geo[0:1, where])
    col_y[0] = columns(down_geo[1:2, where])
    where = at(across[t] * CH)
    build(col_x, col_y, 0, geo[0:1, where], geo[1:2, where], ref, 0)


def fetch(pairs, sems):
    copies = [pltpu.make_async_copy(src, dst, sems.at[k]) for k, (src, dst) in enumerate(pairs)]
    for copy in copies:
        copy.start()
    for copy in copies:
        copy.wait()


def pack_sides(innov, pos_in, sigma_in, count_in, first_out, second_out, pos, sigma, count, sems):
    blocks, members = innov.shape[0], innov.shape[1]
    odd = lax.rem(lax.axis_index("region"), 2)
    starts = ((1 - odd) * (blocks - REACH), odd * (blocks - REACH))
    ends = tuple(zip(starts, (first_out, second_out)))
    pairs = [(pos_in, pos), (sigma_in, sigma), (count_in, count)]
    for start, dst in ends:
        pairs.append((innov.at[pl.ds(start, REACH)], dst.at[:, pl.ds(0, members), :]))
    fetch(pairs, sems)
    for start, dst in ends:
        for b in range(REACH):
            number = jnp.full((1, CH), count[start + b].astype(F32))
            rest = jnp.zeros((4, CH), F32)
            dst[b, members:, :] = jnp.concatenate(
                [pos[start + b], sigma[pl.ds(start + b, 1), :], number, rest], axis=0
            )


def own_kernel(innov_in, pos_in, sigma_in, err_in, count_in, ev, od, vec, geo, acc, ints, floats,
               down, across, innov, pos, sigma, err, count, parts, col_x, col_y, sems):
    blocks = innov.shape[0]
    fetch(
        [(innov_in, innov), (pos_in, pos), (sigma_in, sigma), (err_in, err), (count_in, count)],
        sems,
    )
    acc[...] = jnp.zeros_like(acc)
    origin = pos[0, 0:1, 0:1]

    def pack(b, offset):
        number = count[b]
        ints[b] = offset
        pack_block(innov[b], number, offset, vec)
        pair = pos[b]
        rows = jnp.concatenate(
            [
                (pair[0:1] - origin) * UNIT,
                pair[1:2] * UNIT,
                sigma[pl.ds(b, 1), :],
                err[pl.ds(b, 1), :],
                jnp.zeros((4, CH), F32),
            ],
            axis=0,
        )
        pack_block(rows, number, offset, geo)
        return offset + number

    size = lax.fori_loop(0, blocks, pack, jnp.int32(0))
    ints[blocks] = size
    chunks = (size + CH - 1) // CH
    floats[0] = jnp.max(origin)

    def prepare(i, carry):
        where = at(i * CH)
        x = geo[0:1, where]
        col_x[i] = columns(x)
        col_y[i] = columns(geo[1:2, where])
        put_split(vec[:, where] * geo[2:3, where], parts, i)
        live = lanes((1, CH)) + i * CH < size
        floats[1 + i] = jnp.min(jnp.where(live, x, 3e38))
        floats[1 + blocks + i] = jnp.max(jnp.where(live, x, -3e38))
        return carry

    lax.fori_loop(0, chunks, prepare, 0)

    def enlist(i, t):
        end = floats[1 + blocks + i]
        for d in range(SPAN):
            j = i + d
            start = floats[1 + jnp.minimum(j, blocks - 1)]
            down[t] = i
            across[t] = j
            t = t + jnp.where((j < chunks) & (start - end < LIMIT), 1, 0)
        return t

    total = lax.fori_loop(0, chunks, enlist, jnp.int32(0))
    for extra in range(3):
        down[total + extra] = 0
        across[total + extra] = 0
    ints[blocks + 1] = total

    def make(t, which, slot):
        where = at(across[t] * CH)
        build(col_x, col_y, down[t], geo[0:1, where], geo[1:2, where], (ev, od)[which], slot)

    def multiply(t, which, slot):
        own_product(t, total, down, across, parts, (ev, od)[which], slot, acc)

    sweep(total, ev.shape[0] - 1, make, multiply)


def edge_kernel(from_first, from_second, vec, geo, acc, ints, floats, ev, od, side_geo, side_ints,
                down, across, out, parts, first_out, second_out, side_vec, side_parts, col_x, col_y):
    members = vec.shape[0]
    blocks = (vec.shape[1] - 2 * CH) // CH
    wide = side_vec.shape[1] // 2
    size = ints[blocks]
    chunks = (size + CH - 1) // CH
    origin = floats[0]
    out[...] = jnp.zeros_like(out)
    side_ends = []
    odd = lax.rem(lax.axis_index("region"), 2)
    for side, ref in enumerate((from_first, from_second)):
        offset = jnp.int32(side * wide)
        for b in range(REACH):
            misc = ref[b, members:, :]
            number = misc[3, 0].astype(I32)
            pack_block(ref[b, :members, :], number, offset, side_vec)
            rows = jnp.concatenate(
                [(misc[0:1] - origin) * UNIT, misc[1:2] * UNIT, misc[2:]], axis=0
            )
            pack_block(rows, number, offset, side_geo)
            offset = offset + number
        side_ends.append(offset)
    total = jnp.int32(0)
    down[0] = 0
    across[0] = 0
    for side, end in enumerate(side_ends):
        begin = side * (wide // CH)
        side_chunks = (end - side * wide + CH - 1) // CH

        ahead = odd == side

        def prepare(h, t, begin=begin, end=end, ahead=ahead):
            place = begin + h
            where = at(place * CH)
            x = side_geo[0:1, where]
            col_x[place] = columns(x)
            col_y[place] = columns(side_geo[1:2, where])
            put_split(side_vec[:, where] * side_geo[2:3, where], side_parts, place)
            live = lanes((1, CH)) + place * CH < end
            low = jnp.min(jnp.where(live, x, 3e38))
            high = jnp.max(jnp.where(live, x, -3e38))
            for d in range(SPAN):
                i = jnp.where(ahead, jnp.maximum(chunks - 1 - d, 0), jnp.minimum(d, chunks - 1))
                apart = jnp.where(ahead, low - floats[1 + blocks + i], floats[1 + i] - high)
                down[t] = place
                across[t] = i
                t = t + jnp.where((apart < LIMIT) & (d < chunks), 1, 0)
            return t

        total = lax.fori_loop(0, side_chunks, prepare, total)
    last = jnp.maximum(total - 1, 0)
    for extra in range(3):
        down[total + extra] = down[last]
        across[total + extra] = across[last]
    side_ints[0] = total

    def make(t, which, slot):
        where = at(across[t] * CH)
        build(col_x, col_y, down[t], geo[0:1, where], geo[1:2, where], (ev, od)[which], slot)

    def multiply(t, which, slot):
        edge_product(t, total, down, across, side_parts, (ev, od)[which], slot, out)

    sweep(total, ev.shape[0] - 1, make, multiply)

    def finish(i, carry):
        where = at(i * CH)
        scale = geo[2:3, where]
        image = scale * (out[:, where] + acc[:, where]) + geo[3:4, where] * vec[:, where]
        out[:, where] = image
        put_split(image * scale, parts, i)
        return carry

    lax.fori_loop(0, chunks, finish, 0)
    tail = ints[blocks - REACH]
    for start, dst in (((1 - odd) * tail, first_out), (odd * tail, second_out)):
        base = (start // LN) * LN
        shift = start - base
        back = lax.rem(LN - shift, LN)
        keep = lanes((members, LN)) < LN - shift
        turned = pltpu.roll(out[:, at(base, LN)], back, 1)
        for k in range(REACH * CH // LN):
            following = pltpu.roll(out[:, at(base + (k + 1) * LN, LN)], back, 1)
            dst[:, k * LN : (k + 1) * LN] = jnp.where(keep, turned, following)
            turned = following


def again_kernel(ev, od, parts, geo, ints, down, across, acc, col_x, col_y, ev_more, od_more):
    blocks = acc.shape[1] // CH - 2
    total = ints[blocks + 1]
    held = ev.shape[0] - 1
    acc[...] = jnp.zeros_like(acc)
    more = (ev_more, od_more)

    def multiply(t, which, slot):
        own_product(t, total, down, across, parts, (ev, od)[which], slot, acc)

    sweep(total, held, None, multiply)

    def make_more(t, which, slot):
        remake(t, down, across, geo, geo, col_x, col_y, more[which])

    def multiply_more(t, which, slot):
        own_product(t, total, down, across, parts, more[which], slot, acc)

    sweep_rest(total, held, make_more, multiply_more)


def lane_sum(values):
    return jnp.sum(values, axis=1, keepdims=True)


def last_kernel(from_first, from_second, side_geo, side_ints, ev, od, down, across, acc, vec, image, geo,
                ints, out, sums, side_parts, total_ref, col_x, col_y, ev_more, od_more):
    members = vec.shape[0]
    blocks = vec.shape[1] // CH - 2
    chunks = (ints[blocks] + CH - 1) // CH
    total = side_ints[0]
    total_ref[...] = acc[...]
    per_side = side_geo.shape[1] // CH // 2
    for side, ref in enumerate((from_first, from_second)):
        for h in range(REACH):
            place = side * per_side + h
            scale = side_geo[2:3, place * CH : (place + 1) * CH]
            scaled = jnp.where(scale > 0, ref[:, h * CH : (h + 1) * CH] * scale, 0.0)
            put_split(scaled, side_parts, place)

    held = ev.shape[0] - 1
    more = (ev_more, od_more)

    def multiply(t, which, slot):
        edge_product(t, total, down, across, side_parts, (ev, od)[which], slot, total_ref)

    sweep(total, held, None, multiply)

    def make_more(t, which, slot):
        remake(t, down, across, side_geo, geo, col_x, col_y, more[which])

    def multiply_more(t, which, slot):
        edge_product(t, total, down, across, side_parts, more[which], slot, total_ref)

    sweep_rest(total, held, make_more, multiply_more)
    out[...] = jnp.zeros_like(out)
    zero = jnp.zeros((members, 1), F32)

    def first(i, carry):
        m0, m1 = carry
        where = at(i * CH)
        r, y = vec[:, where], image[:, where]
        out[:, where] = geo[2:3, where] * total_ref[:, where] + geo[3:4, where] * y
        return m0 + lane_sum(r * r), m1 + lane_sum(r * y)

    m0, m1 = lax.fori_loop(0, chunks, first, (zero, zero))
    mean = jnp.where(m0 > 0, m1 / jnp.where(m0 > 0, m0, 1.0), 0.0)

    def second(i, carry):
        vv, zu, cross, slip = carry
        where = at(i * CH)
        r, y = vec[:, where], image[:, where]
        z = y - mean * r
        u = out[:, where] - mean * y
        return (
            vv + lane_sum(z * z),
            zu + lane_sum(z * u),
            cross + lane_sum(z * y + r * u),
            slip + lane_sum(z * r),
        )

    found = lax.fori_loop(0, chunks, second, (zero, zero, zero, zero))
    table = jnp.zeros((members, LN), F32)
    lane = lanes((members, LN))
    for k, value in enumerate((m0, m1, mean) + tuple(found)):
        table = jnp.where(lane == k, value, table)
    turned = jnp.concatenate([table, jnp.zeros((LN - members, LN), F32)], axis=0).T[:8]
    for k in range(sums.shape[0]):
        sums[k] = turned


def update_kernel(sums, vec, image, second, ints, count, solution_out, residual_out, solution_ref,
                  residual_ref, sems):
    members = vec.shape[0]
    blocks = vec.shape[1] // CH - 2
    chunks = (ints[blocks] + CH - 1) // CH
    terms = sums[...]
    m0 = jnp.sum(terms[:, 0, :], axis=0, keepdims=True)
    m1 = jnp.sum(terms[:, 1, :], axis=0, keepdims=True)
    used = lanes((1, LN)) < members
    m0 = jnp.where(used, m0, 1.0)
    m1 = jnp.where(used, m1, 1.0)
    mean = m1 / m0
    off = mean - terms[:, 2, :]
    vv = terms[:, 3, :] - 2.0 * off * terms[:, 6, :] + off * off * terms[:, 0, :]
    zu = terms[:, 4, :] - off * terms[:, 5, :] + off * off * terms[:, 1, :]
    cross = terms[:, 5, :] - 2.0 * off * terms[:, 1, :]
    vv, zu, cross = (jnp.sum(x, axis=0, keepdims=True) for x in (vv, zu, cross))
    alpha = m0 / m1
    rr = alpha * alpha * vv
    beta = rr / m0
    alpha_next = rr / (alpha * alpha * zu - alpha * beta * cross + beta * beta * m1)
    one = alpha + alpha_next * (1.0 + beta)
    two = alpha * alpha_next
    table = jnp.concatenate([one, two, jnp.zeros((LN - 2, LN), F32)], axis=0).T
    one, two = table[:members, 0:1], table[:members, 1:2]

    copies = []
    lane = lanes((2 * members, LN))
    for b in range(blocks):
        offset, number = ints[b], count[b]
        base = (offset // LN) * LN
        shift = offset - base
        back = lax.rem(LN - shift, LN)
        keep = lane < LN - shift
        turned = []
        for k in range(3):
            where = at(base + k * LN, LN)
            r, y, yy = vec[:, where], image[:, where], second[:, where]
            both = jnp.concatenate([one * r - two * y, r - one * y + two * yy], axis=0)
            turned.append(pltpu.roll(both, back, 1))
        for k in range(2):
            part = jnp.where(keep, turned[k], turned[k + 1])
            part = jnp.where(lane + k * LN < number, part, 0.0)
            solution_ref[b, :, k * LN : (k + 1) * LN] = part[:members]
            residual_ref[b, :, k * LN : (k + 1) * LN] = part[members:]
        for k, (src, dst) in enumerate(((solution_ref, solution_out), (residual_ref, residual_out))):
            copy = pltpu.make_async_copy(src.at[b], dst.at[b], sems.at[k, b])
            copy.start()
            copies.append(copy)
    for copy in copies:
        copy.wait()


def exchange(first, second):
    devices = lax.axis_size("region")
    received = []
    for start, block in enumerate((first, second)):
        pairs = [(i, i + 1) for i in range(start, devices - 1, 2)]
        received.append(lax.ppermute(block, "region", pairs + [(b, a) for a, b in pairs]))
    return received


def call(kernel, name, in_specs, outs, scratch=(), limit=9 * MB, cost=None):
    return pl.pallas_call(
        kernel,
        name=name,
        in_specs=in_specs,
        out_specs=[spec for spec, _ in outs],
        out_shape=[shape for _, shape in outs],
        scratch_shapes=list(scratch),
        compiler_params=pltpu.CompilerParams(vmem_limit_bytes=limit),
        cost_estimate=cost,
    )


def body(obs_pos, obs_sigma, obs_error, innovation, obs_count, pair_list, pair_live):
    blocks, members, _ = innovation.shape
    sd = jax.ShapeDtypeStruct
    in_hbm = functools.partial(pltpu.with_memory_space_constraint, memory_space=pltpu.HBM)
    in_vmem = functools.partial(pltpu.with_memory_space_constraint, memory_space=pltpu.VMEM)
    wide = blocks * CH + 2 * CH
    side_chunks = REACH + 2
    own_slots, side_slots = OWN_HELD // 2 + 1, SIDE_HELD // 2 + 1
    listed = blocks * SPAN + 16
    pack_out = (VM, sd((REACH, members + 8, CH), F32))
    again_scratch = [
        pltpu.VMEM((1, CH, LN), F32),
        pltpu.VMEM((1, CH, LN), F32),
        pltpu.VMEM((1, 2 * CH, CH), BF16),
        pltpu.VMEM((1, 2 * CH, CH), BF16),
    ]
    sides = call(
        pack_sides, "pack", [HB] * 4, [pack_out, pack_out],
        [
            pltpu.VMEM(obs_pos.shape, F32),
            pltpu.VMEM(obs_sigma.shape, F32),
            pltpu.SMEM(obs_count.shape, I32),
            pltpu.SemaphoreType.DMA((5,)),
        ],
        limit=3 * MB,
    )(*map(in_hbm, (innovation, obs_pos, obs_sigma, obs_count)))
    sides = exchange(*sides)
    dense = (VM, sd((members, wide), F32))
    tile = (2 * CH, CH)
    ev, od, vec, geo, acc, ints, floats, down, across = call(
        own_kernel, "own", [HB] * 5,
        [
            (VM, pltpu.VMEM((own_slots,) + tile, BF16)),
            (VM, pltpu.VMEM((own_slots,) + tile, BF16)),
            dense,
            (VM, sd((8, wide), F32)),
            dense,
            (SM, sd((blocks + 2,), I32)),
            (SM, sd((2 * blocks + 1,), F32)),
            (SM, sd((listed,), I32)),
            (SM, sd((listed,), I32)),
        ],
        [
            pltpu.VMEM(innovation.shape, F32),
            pltpu.VMEM(obs_pos.shape, F32),
            pltpu.VMEM(obs_sigma.shape, F32),
            pltpu.VMEM(obs_error.shape, F32),
            pltpu.SMEM(obs_count.shape, I32),
            pltpu.VMEM((blocks, 2 * members, CH), BF16),
            pltpu.VMEM((blocks, CH, LN), F32),
            pltpu.VMEM((blocks, CH, LN), F32),
            pltpu.SemaphoreType.DMA((5,)),
        ],
        cost=pl.CostEstimate(flops=4 * 10**9, bytes_accessed=20 * MB, transcendentals=0),
    )(*map(in_hbm, (innovation, obs_pos, obs_sigma, obs_error, obs_count)))
    ev, od = in_vmem(ev), in_vmem(od)
    side = (VM, sd((members, REACH * CH), F32))
    (side_ev, side_od, side_geo, side_ints, side_down, side_across, image, parts,
     *image_sides) = call(
        edge_kernel, "edge", [VM, VM, VM, VM, VM, SM, SM],
        [
            (VM, pltpu.VMEM((side_slots,) + tile, BF16)),
            (VM, pltpu.VMEM((side_slots,) + tile, BF16)),
            (VM, sd((8, 2 * side_chunks * CH), F32)),
            (SM, sd((1,), I32)),
            (SM, sd((128,), I32)),
            (SM, sd((128,), I32)),
            dense,
            (VM, sd((blocks, 2 * members, CH), BF16)),
            side,
            side,
        ],
        [
            pltpu.VMEM((members, 2 * side_chunks * CH), F32),
            pltpu.VMEM((2 * side_chunks, 2 * members, CH), BF16),
            pltpu.VMEM((2 * side_chunks, CH, LN), F32),
            pltpu.VMEM((2 * side_chunks, CH, LN), F32),
        ],
        limit=7 * MB,
    )(*sides, vec, geo, acc, ints, floats)
    side_ev, side_od = in_vmem(side_ev), in_vmem(side_od)
    image_sides = exchange(*image_sides)
    (acc,) = call(
        again_kernel, "again", [VM, VM, VM, VM, SM, SM, SM], [dense], again_scratch, limit=3 * MB,
        cost=pl.CostEstimate(flops=4 * 10**9, bytes_accessed=20 * MB, transcendentals=0),
    )(ev, od, parts, geo, ints, down, across)
    devices = lax.axis_size("region")
    second, sums = call(
        last_kernel, "last", [VM, VM, VM, SM, VM, VM, SM, SM, VM, VM, VM, VM, SM],
        [dense, (VM, sd((devices, 8, LN), F32))],
        [
            pltpu.VMEM((2 * side_chunks, 2 * members, CH), BF16),
            pltpu.VMEM((members, wide), F32),
            *again_scratch,
        ],
        limit=5 * MB,
    )(*image_sides, side_geo, side_ints, side_ev, side_od, side_down, side_across,
      acc, vec, image, geo, ints)
    sums = lax.all_to_all(sums, "region", 0, 0)
    field = (HB, sd((blocks, members, CH), F32))
    return tuple(call(
        update_kernel, "update", [VM, VM, VM, VM, SM, SM], [field, field],
        [
            pltpu.VMEM((blocks, members, CH), F32),
            pltpu.VMEM((blocks, members, CH), F32),
            pltpu.SemaphoreType.DMA((2, blocks)),
        ],
        limit=6 * MB,
    )(sums, vec, image, second, ints, obs_count))


def solution(mesh):
    return jax.shard_map(
        body,
        mesh=mesh,
        in_specs=(
            P(("groups", "region"), None, None),
            P(("groups", "region"), None),
            P(("groups", "region"), None),
            P(("groups", "region"), None, None),
            P(("groups", "region")),
            P(None, ("groups", "region")),
            P(("groups", "region")),
        ),
        out_specs=(P(("groups", "region"), None, None), P(("groups", "region"), None, None)),
        check_vma=False,
    )
```

```python
import functools

import jax
import jax.numpy as jnp
from jax import lax
from jax.experimental import pallas as pl
from jax.experimental.pallas import tpu as pltpu
from jax.sharding import PartitionSpec as P

REACH = 5
CUTOFF_KM = 1500.0
SCALE_KM = 1000.0
LOG2E = 1.4426950408889634
UNIT = LOG2E / SCALE_KM
TAPER = 1.0 / (CUTOFF_KM * UNIT)
LIMIT = CUTOFF_KM * UNIT
CH = 256
LN = 128
GROUP = 4
BATCH = 8
SPAN = 7
TINY = 1e-30
F32, BF16, I32 = jnp.float32, jnp.bfloat16, jnp.int32
VM = pl.BlockSpec(memory_space=pltpu.VMEM)
SM = pl.BlockSpec(memory_space=pltpu.SMEM)
HB = pl.BlockSpec(memory_space=pltpu.HBM)
MB = 1 << 20
OWN_HELD = 56
SIDE_HELD = 24


def lanes(shape):
    return lax.broadcasted_iota(I32, shape, len(shape) - 1)


def at(start, size=CH):
    return pl.ds(pl.multiple_of(start, LN), size)


def pack_block(rows, count, offset, dst):
    base = (offset // LN) * LN
    shift = offset - base
    lane = lanes((rows.shape[0], LN))
    low = pltpu.roll(jnp.where(lane < count, rows[:, :LN], 0.0), shift, 1)
    high = pltpu.roll(jnp.where(lane + LN < count, rows[:, LN:], 0.0), shift, 1)
    before = lane < shift
    dst[:, at(base, LN)] = jnp.where(before, dst[:, at(base, LN)], low)
    dst[:, at(base + LN, LN)] = jnp.where(before, low, high)
    dst[:, at(base + 2 * LN, LN)] = jnp.where(before, high, 0.0)
    dst[:, at(base + 3 * LN, LN)] = jnp.zeros_like(low)


def split(values):
    high = values.astype(BF16)
    return high, (values - high.astype(F32)).astype(BF16)


def put_split(values, dst, place):
    high, low = split(values)
    half = values.shape[0]
    dst[place, :half, :] = high
    dst[place, half:, :] = low


def columns(row):
    parts = [jnp.broadcast_to(row[:, k : k + LN], (LN, LN)).T for k in (0, LN)]
    return jnp.concatenate(parts, axis=0)


def build(col_x, col_y, place, row_x, row_y, tile_ref, slot):
    strip = 32
    for top in range(0, CH, strip):
        for left in range(0, CH, LN):
            dx = col_x[place, top : top + strip, :] - row_x[:, left : left + LN]
            dy = col_y[place, top : top + strip, :] - row_y[:, left : left + LN]
            square = jnp.maximum(dx * dx + dy * dy, TINY)
            distance = square * lax.rsqrt(square)
            tapered = jnp.maximum(1.0 - distance * TAPER, 0.0)
            value = jnp.exp2(-distance) * (tapered * tapered)
            high, low = split(value)
            tile_ref[slot, top : top + strip, left : left + LN] = high
            tile_ref[slot, CH + top : CH + top + strip, left : left + LN] = low


def product(parts_ref, place, tile_ref, slot, transposed):
    dims = (((1,), (1 if transposed else 0,)), ((), ()))
    both = parts_ref[place]
    half = both.shape[0] // 2
    wide = lax.dot_general(both, tile_ref[slot, :CH, :], dims, preferred_element_type=F32)
    fine = lax.dot_general(both[:half], tile_ref[slot, CH:, :], dims, preferred_element_type=F32)
    return wide[:half] + wide[half:] + fine


def own_product(t, total, down, across, parts_ref, tile_ref, slot, acc):
    i, j = down[t], across[t]
    here = (t < total).astype(F32)
    forward = product(parts_ref, i, tile_ref, slot, False)
    backward = product(parts_ref, j, tile_ref, slot, True)
    acc[:, at(j * CH)] += here * forward
    acc[:, at(i * CH)] += here * backward


def diagonal_product(t, total, parts_ref, tile_ref, slot, acc):
    here = (t < total).astype(F32)
    i = jnp.minimum(t, total - 1)
    acc[:, at(i * CH)] += here * product(parts_ref, i, tile_ref, slot, False)


def edge_product(t, total, down, across, parts_ref, tile_ref, slot, acc):
    here = (t < total).astype(F32)
    acc[:, at(across[t] * CH)] += here * product(parts_ref, down[t], tile_ref, slot, False)


def sweep(total, held, make, multiply):
    pairs = (total + 1) // 2
    full = jnp.minimum(total, 2 * held) // BATCH

    def many(p, carry):
        for half in (make, multiply):
            for u in range(BATCH):
                if half is not None:
                    half(BATCH * p + u, u % 2, BATCH // 2 * p + u // 2)
        return carry

    def few(p, carry):
        for half in (make, multiply):
            for u in range(2):
                if half is not None:
                    half(2 * p + u, u, jnp.minimum(p, held))
        return carry

    lax.fori_loop(0, full, many, 0)
    end = pairs if make is not None else jnp.minimum(pairs, held)
    lax.fori_loop(full * (BATCH // 2), end, few, 0)


def sweep_rest(total, held, make, multiply):
    def few(p, carry):
        for half in (make, multiply):
            for u in range(2):
                half(2 * p + u, u, 0)
        return carry

    lax.fori_loop(held, (total + 1) // 2, few, 0)


def remake(t, down, across, down_geo, geo, col_x, col_y, ref):
    where = at(down[t] * CH)
    col_x[0] = columns(down_geo[0:1, where])
    col_y[0] = columns(down_geo[1:2, where])
    where = at(across[t] * CH)
    build(col_x, col_y, 0, geo[0:1, where], geo[1:2, where], ref, 0)


def prepare_kernel(innov_in, pos_in, sigma_in, err_in, count_in, first_out, second_out, vec, geo,
                   parts, col_x, col_y, ints, floats, down, across, innov, pos, sigma, err, count,
                   sems):
    blocks, members = innov.shape[0], innov.shape[1]
    odd = lax.rem(lax.axis_index("region"), 2)
    starts = ((1 - odd) * (blocks - REACH), odd * (blocks - REACH))
    ends = tuple(zip(starts, (first_out, second_out)))
    small = [(pos_in, pos), (sigma_in, sigma), (err_in, err), (count_in, count)]
    large = [(innov_in, innov)]
    for start, dst in ends:
        large.append((innov_in.at[pl.ds(start, REACH)], dst.at[:, pl.ds(0, members), :]))
    copies = [
        pltpu.make_async_copy(src, dst, sems.at[k]) for k, (src, dst) in enumerate(small + large)
    ]
    for copy in copies:
        copy.start()
    for copy in copies[: len(small)]:
        copy.wait()
    for start, dst in ends:
        for b in range(REACH):
            number = jnp.full((1, CH), count[start + b].astype(F32))
            rest = jnp.zeros((4, CH), F32)
            dst[b, members:, :] = jnp.concatenate(
                [pos[start + b], sigma[pl.ds(start + b, 1), :], number, rest], axis=0
            )
    origin = pos[0, 0:1, 0:1]
    floats[0] = jnp.max(origin)

    def pack_geo(b, offset):
        ints[b] = offset
        pair = pos[b]
        rows = jnp.concatenate(
            [
                (pair[0:1] - origin) * UNIT,
                pair[1:2] * UNIT,
                sigma[pl.ds(b, 1), :],
                err[pl.ds(b, 1), :],
                jnp.zeros((4, CH), F32),
            ],
            axis=0,
        )
        pack_block(rows, count[b], offset, geo)
        return offset + count[b]

    size = lax.fori_loop(0, blocks, pack_geo, jnp.int32(0), unroll=4)
    ints[blocks] = size
    chunks = (size + CH - 1) // CH
    for copy in copies[len(small) :]:
        copy.wait()

    def pack_vec(b, carry):
        pack_block(innov[b], count[b], ints[b], vec)
        return carry

    lax.fori_loop(0, blocks, pack_vec, 0, unroll=4)

    def prepare(p, carry):
        for u in range(GROUP):
            i = p * GROUP + u
            where = at(i * CH)
            x = geo[0:1, where]
            col_x[i] = columns(x)
            col_y[i] = columns(geo[1:2, where])
            put_split(vec[:, where] * geo[2:3, where], parts, i)
            live = lanes((1, CH)) + i * CH < size
            floats[1 + i] = jnp.min(jnp.where(live, x, 3e38))
            floats[1 + blocks + i] = jnp.max(jnp.where(live, x, -3e38))
        return carry

    lax.fori_loop(0, (chunks + GROUP - 1) // GROUP, prepare, 0)

    def enlist(i, t):
        end = floats[1 + blocks + i]
        for d in range(1, SPAN):
            j = i + d
            start = floats[1 + jnp.minimum(j, blocks - 1)]
            down[t] = i
            across[t] = j
            t = t + jnp.where((j < chunks) & (start - end < LIMIT), 1, 0)
        return t

    total = lax.fori_loop(0, chunks, enlist, jnp.int32(0))
    down[total] = 0
    across[total] = 0
    ints[blocks + 1] = total


def own_kernel(geo, parts, col_x, col_y, ints, down, across, diagonal_ev, diagonal_od, ev, od, acc):
    blocks = parts.shape[0]
    chunks = (ints[blocks] + CH - 1) // CH
    total = ints[blocks + 1]
    acc[...] = jnp.zeros_like(acc)

    def build_at(i, j, ref, slot):
        where = at(j * CH)
        build(col_x, col_y, i, geo[0:1, where], geo[1:2, where], ref, slot)

    def make_diagonal(t, which, slot):
        i = jnp.minimum(t, chunks - 1)
        build_at(i, i, (diagonal_ev, diagonal_od)[which], slot)

    def multiply_diagonal(t, which, slot):
        diagonal_product(t, chunks, parts, (diagonal_ev, diagonal_od)[which], slot, acc)

    sweep(chunks, blocks // 2, make_diagonal, multiply_diagonal)

    def make(t, which, slot):
        build_at(down[t], across[t], (ev, od)[which], slot)

    def multiply(t, which, slot):
        own_product(t, total, down, across, parts, (ev, od)[which], slot, acc)

    sweep(total, ev.shape[0] - 1, make, multiply)


def edge_kernel(from_first, from_second, vec, geo, acc, ints, floats, ev, od, side_geo, side_ints,
                down, across, out, parts, first_out, second_out, side_vec, side_parts, col_x, col_y,
                floats_side):
    members = vec.shape[0]
    blocks = (vec.shape[1] - 2 * CH) // CH
    wide = side_vec.shape[1] // 2
    size = ints[blocks]
    chunks = (size + CH - 1) // CH
    origin = floats[0]
    out[...] = jnp.zeros_like(out)
    side_ends = []
    odd = lax.rem(lax.axis_index("region"), 2)
    for side, ref in enumerate((from_first, from_second)):
        offset = jnp.int32(side * wide)
        for b in range(REACH):
            misc = ref[b, members:, :]
            number = misc[3, 0].astype(I32)
            pack_block(ref[b, :members, :], number, offset, side_vec)
            rows = jnp.concatenate(
                [(misc[0:1] - origin) * UNIT, misc[1:2] * UNIT, misc[2:]], axis=0
            )
            pack_block(rows, number, offset, side_geo)
            offset = offset + number
        side_ends.append(offset)
    down[0] = 0
    across[0] = 0
    side_chunks = [(end - k * wide + CH - 1) // CH for k, end in enumerate(side_ends)]

    def prepare(p, t):
        for h, side in ((2 * p, 0), (2 * p, 1), (2 * p + 1, 0), (2 * p + 1, 1)):
            place = side * (wide // CH) + h
            where = at(place * CH)
            x = side_geo[0:1, where]
            col_x[place] = columns(x)
            col_y[place] = columns(side_geo[1:2, where])
            put_split(side_vec[:, where] * side_geo[2:3, where], side_parts, place)
            live = lanes((1, CH)) + place * CH < side_ends[side]
            floats_side[2 * place] = jnp.min(jnp.where(live, x, 3e38))
            floats_side[2 * place + 1] = jnp.max(jnp.where(live, x, -3e38))
        return t

    lax.fori_loop(0, (jnp.maximum(*side_chunks) + 1) // 2, prepare, 0)
    total = jnp.int32(0)
    for side in range(2):
        ahead = odd == side

        def enlist(h, t, side=side, ahead=ahead):
            place = side * (wide // CH) + h
            low, high = floats_side[2 * place], floats_side[2 * place + 1]
            for d in range(SPAN):
                i = jnp.where(ahead, jnp.maximum(chunks - 1 - d, 0), jnp.minimum(d, chunks - 1))
                apart = jnp.where(ahead, low - floats[1 + blocks + i], floats[1 + i] - high)
                down[t] = place
                across[t] = i
                t = t + jnp.where((apart < LIMIT) & (d < chunks), 1, 0)
            return t

        total = lax.fori_loop(0, side_chunks[side], enlist, total)
    last = jnp.maximum(total - 1, 0)
    down[total] = down[last]
    across[total] = across[last]
    side_ints[0] = total
    for side in range(2):
        side_ints[1 + side] = side_chunks[side]

    def make(t, which, slot):
        where = at(across[t] * CH)
        build(col_x, col_y, down[t], geo[0:1, where], geo[1:2, where], (ev, od)[which], slot)

    def multiply(t, which, slot):
        edge_product(t, total, down, across, side_parts, (ev, od)[which], slot, out)

    sweep(total, ev.shape[0] - 1, make, multiply)

    def finish(i, carry):
        where = at(i * CH)
        scale = geo[2:3, where]
        image = scale * (out[:, where] + acc[:, where]) + geo[3:4, where] * vec[:, where]
        out[:, where] = image
        put_split(image * scale, parts, i)
        return carry

    lax.fori_loop(0, chunks, finish, 0)
    tail = ints[blocks - REACH]
    for start, dst in (((1 - odd) * tail, first_out), (odd * tail, second_out)):
        base = (start // LN) * LN
        shift = start - base
        back = lax.rem(LN - shift, LN)
        keep = lanes((members, LN)) < LN - shift
        turned = pltpu.roll(out[:, at(base, LN)], back, 1)
        for k in range(REACH * CH // LN):
            following = pltpu.roll(out[:, at(base + (k + 1) * LN, LN)], back, 1)
            dst[:, k * LN : (k + 1) * LN] = jnp.where(keep, turned, following)
            turned = following


def halves(values):
    return values[:, :LN] + values[:, LN:]


def lane_sum(values):
    return jnp.sum(values, axis=1, keepdims=True)


def again_kernel(diagonal_ev, diagonal_od, ev, od, parts, geo, vec, image, ints, down, across, acc,
                 known, col_x, col_y, ev_more, od_more):
    blocks = acc.shape[1] // CH - 2
    total = ints[blocks + 1]
    held = ev.shape[0] - 1
    acc[...] = jnp.zeros_like(acc)
    more = (ev_more, od_more)
    chunks = (ints[blocks] + CH - 1) // CH

    def multiply_diagonal(t, which, slot):
        diagonal_product(t, chunks, parts, (diagonal_ev, diagonal_od)[which], slot, acc)

    sweep(chunks, blocks // 2, None, multiply_diagonal)

    def multiply(t, which, slot):
        own_product(t, total, down, across, parts, (ev, od)[which], slot, acc)

    sweep(total, held, None, multiply)

    def make_more(t, which, slot):
        remake(t, down, across, geo, geo, col_x, col_y, more[which])

    def multiply_more(t, which, slot):
        own_product(t, total, down, across, parts, more[which], slot, acc)

    sweep_rest(total, held, make_more, multiply_more)
    members = vec.shape[0]
    zero = jnp.zeros((members, LN), F32)

    def first(i, carry):
        m0, m1 = carry
        r, y = vec[:, at(i * CH)], image[:, at(i * CH)]
        return m0 + halves(r * r), m1 + halves(r * y)

    m0, m1 = (lane_sum(x) for x in lax.fori_loop(0, chunks, first, (zero, zero)))
    mean = jnp.where(m0 > 0, m1 / jnp.where(m0 > 0, m0, 1.0), 0.0)

    def second(i, carry):
        vv, cross, slip = carry
        r, y = vec[:, at(i * CH)], image[:, at(i * CH)]
        z = y - mean * r
        return vv + halves(z * z), cross + halves(z * y), slip + halves(z * r)

    vv, cross, slip = (lane_sum(x) for x in lax.fori_loop(0, chunks, second, (zero, zero, zero)))
    table = jnp.zeros((members, LN), F32)
    lane = lanes((members, LN))
    for k, value in ((0, m0), (1, m1), (2, mean), (3, vv), (5, cross), (6, slip)):
        table = jnp.where(lane == k, value, table)
    known[...] = table


def last_kernel(from_first, from_second, side_geo, side_ints, ev, od, down, across, acc, known, vec,
                image, geo, ints, out, sums, side_parts, total_ref, col_x, col_y, ev_more, od_more):
    members = vec.shape[0]
    blocks = vec.shape[1] // CH - 2
    chunks = (ints[blocks] + CH - 1) // CH
    total = side_ints[0]
    per_side = side_geo.shape[1] // CH // 2

    def carry_over(i, carry):
        total_ref[:, at(i * CH)] = acc[:, at(i * CH)]
        return carry

    lax.fori_loop(0, chunks, carry_over, 0)
    for side, ref in enumerate((from_first, from_second)):

        def scale_side(h, carry, side=side, ref=ref):
            place = side * per_side + h
            scale = side_geo[2:3, at(place * CH)]
            put_split(ref[:, at(h * CH)] * scale, side_parts, place)
            return carry

        lax.fori_loop(0, side_ints[1 + side], scale_side, 0)
    held = ev.shape[0] - 1
    more = (ev_more, od_more)

    def multiply(t, which, slot):
        edge_product(t, total, down, across, side_parts, (ev, od)[which], slot, total_ref)

    sweep(total, held, None, multiply)

    def make_more(t, which, slot):
        remake(t, down, across, side_geo, geo, col_x, col_y, more[which])

    def multiply_more(t, which, slot):
        edge_product(t, total, down, across, side_parts, more[which], slot, total_ref)

    sweep_rest(total, held, make_more, multiply_more)
    zero = jnp.zeros((members, LN), F32)
    mean = known[:, 2:3]
    tail = jnp.zeros((members, 2 * LN), F32)
    for k in range(2):
        out[:, at((chunks + k) * CH)] = tail

    def sums_of(i, carry):
        zu, cross = carry
        where = at(i * CH)
        r, y = vec[:, where], image[:, where]
        yy = geo[2:3, where] * total_ref[:, where] + geo[3:4, where] * y
        out[:, where] = yy
        u = yy - mean * y
        return zu + halves((y - mean * r) * u), cross + halves(r * u)

    zu, cross = (lane_sum(x) for x in lax.fori_loop(0, chunks, sums_of, (zero, zero)))
    lane = lanes((members, LN))
    table = known[...]
    table = jnp.where(lane == 4, zu, table)
    table = jnp.where(lane == 5, cross + table, table)
    turned = jnp.concatenate([table, jnp.zeros((LN - members, LN), F32)], axis=0).T[:8]
    for k in range(sums.shape[0]):
        sums[k] = turned


def update_kernel(sums, vec, image, second, ints, count, solution_out, residual_out, solution_ref,
                  residual_ref, sems):
    members = vec.shape[0]
    blocks = vec.shape[1] // CH - 2
    chunks = (ints[blocks] + CH - 1) // CH
    terms = sums[...]
    m0 = jnp.sum(terms[:, 0, :], axis=0, keepdims=True)
    m1 = jnp.sum(terms[:, 1, :], axis=0, keepdims=True)
    used = lanes((1, LN)) < members
    m0 = jnp.where(used, m0, 1.0)
    m1 = jnp.where(used, m1, 1.0)
    mean = m1 / m0
    off = mean - terms[:, 2, :]
    vv = terms[:, 3, :] - 2.0 * off * terms[:, 6, :] + off * off * terms[:, 0, :]
    zu = terms[:, 4, :] - off * terms[:, 5, :] + off * off * terms[:, 1, :]
    cross = terms[:, 5, :] - 2.0 * off * terms[:, 1, :]
    vv, zu, cross = (jnp.sum(x, axis=0, keepdims=True) for x in (vv, zu, cross))
    alpha = m0 / m1
    rr = alpha * alpha * vv
    beta = rr / m0
    alpha_next = rr / (alpha * alpha * zu - alpha * beta * cross + beta * beta * m1)
    one = alpha + alpha_next * (1.0 + beta)
    two = alpha * alpha_next
    table = jnp.concatenate([one, two, jnp.zeros((LN - 2, LN), F32)], axis=0).T
    one, two = table[:members, 0:1], table[:members, 1:2]

    copies = []
    lane = lanes((2 * members, LN))
    for b in range(blocks):
        offset, number = ints[b], count[b]
        base = (offset // LN) * LN
        shift = offset - base
        back = lax.rem(LN - shift, LN)
        keep = lane < LN - shift
        turned = []
        for k in range(3):
            where = at(base + k * LN, LN)
            r, y, yy = vec[:, where], image[:, where], second[:, where]
            both = jnp.concatenate([one * r - two * y, r - one * y + two * yy], axis=0)
            turned.append(pltpu.roll(both, back, 1))
        for k in range(2):
            part = jnp.where(keep, turned[k], turned[k + 1])
            part = jnp.where(lane + k * LN < number, part, 0.0)
            solution_ref[b, :, k * LN : (k + 1) * LN] = part[:members]
            residual_ref[b, :, k * LN : (k + 1) * LN] = part[members:]
        for k, (src, dst) in enumerate(((solution_ref, solution_out), (residual_ref, residual_out))):
            copy = pltpu.make_async_copy(src.at[b], dst.at[b], sems.at[k, b])
            copy.start()
            copies.append(copy)
    for copy in copies:
        copy.wait()


def exchange(first, second):
    devices = lax.axis_size("region")
    received = []
    for start, block in enumerate((first, second)):
        pairs = [(i, i + 1) for i in range(start, devices - 1, 2)]
        received.append(lax.ppermute(block, "region", pairs + [(b, a) for a, b in pairs]))
    return received


def call(kernel, name, in_specs, outs, scratch=(), limit=9 * MB, cost=None):
    return pl.pallas_call(
        kernel,
        name=name,
        in_specs=in_specs,
        out_specs=[spec for spec, _ in outs],
        out_shape=[shape for _, shape in outs],
        scratch_shapes=list(scratch),
        compiler_params=pltpu.CompilerParams(vmem_limit_bytes=limit),
        cost_estimate=cost,
    )


def body(obs_pos, obs_sigma, obs_error, innovation, obs_count, pair_list, pair_live):
    blocks, members, _ = innovation.shape
    sd = jax.ShapeDtypeStruct
    in_hbm = functools.partial(pltpu.with_memory_space_constraint, memory_space=pltpu.HBM)
    in_vmem = functools.partial(pltpu.with_memory_space_constraint, memory_space=pltpu.VMEM)
    wide = blocks * CH + 2 * CH
    side_chunks = REACH + 2
    own_slots = [blocks // 2 + 1] * 2 + [OWN_HELD // 2 + 1] * 2
    side_slots = SIDE_HELD // 2 + 1
    listed = blocks * SPAN + 16
    pack_out = (VM, sd((REACH, members + 8, CH), F32))
    again_scratch = [
        pltpu.VMEM((1, CH, LN), F32),
        pltpu.VMEM((1, CH, LN), F32),
        pltpu.VMEM((1, 2 * CH, CH), BF16),
        pltpu.VMEM((1, 2 * CH, CH), BF16),
    ]
    dense = (VM, sd((members, wide), F32))
    tile = (2 * CH, CH)
    column = (VM, sd((blocks, CH, LN), F32))
    *sides, vec, geo, parts, col_x, col_y, ints, floats, down, across = call(
        prepare_kernel, "prepare", [HB] * 5,
        [
            pack_out,
            pack_out,
            dense,
            (VM, sd((8, wide), F32)),
            (VM, sd((blocks, 2 * members, CH), BF16)),
            column,
            column,
            (SM, sd((blocks + 2,), I32)),
            (SM, sd((2 * blocks + 1,), F32)),
            (SM, sd((listed,), I32)),
            (SM, sd((listed,), I32)),
        ],
        [
            pltpu.VMEM(innovation.shape, F32),
            pltpu.VMEM(obs_pos.shape, F32),
            pltpu.VMEM(obs_sigma.shape, F32),
            pltpu.VMEM(obs_error.shape, F32),
            pltpu.SMEM(obs_count.shape, I32),
            pltpu.SemaphoreType.DMA((7,)),
        ],
        limit=9 * MB,
    )(*map(in_hbm, (innovation, obs_pos, obs_sigma, obs_error, obs_count)))
    sides = exchange(*sides)
    *tiles, acc = call(
        own_kernel, "own", [VM, VM, VM, VM, SM, SM, SM],
        [(VM, pltpu.VMEM((slots,) + tile, BF16)) for slots in own_slots] + [dense],
        limit=6 * MB,
        cost=pl.CostEstimate(flops=4 * 10**9, bytes_accessed=20 * MB, transcendentals=0),
    )(geo, parts, col_x, col_y, ints, down, across)
    tiles = map(in_vmem, tiles)
    side = (VM, sd((members, REACH * CH), F32))
    (side_ev, side_od, side_geo, side_ints, side_down, side_across, image, parts,
     *image_sides) = call(
        edge_kernel, "edge", [VM, VM, VM, VM, VM, SM, SM],
        [
            (VM, pltpu.VMEM((side_slots,) + tile, BF16)),
            (VM, pltpu.VMEM((side_slots,) + tile, BF16)),
            (VM, sd((8, 2 * side_chunks * CH), F32)),
            (SM, sd((3,), I32)),
            (SM, sd((128,), I32)),
            (SM, sd((128,), I32)),
            dense,
            (VM, sd((blocks, 2 * members, CH), BF16)),
            side,
            side,
        ],
        [
            pltpu.VMEM((members, 2 * side_chunks * CH), F32),
            pltpu.VMEM((2 * side_chunks, 2 * members, CH), BF16),
            pltpu.VMEM((2 * side_chunks, CH, LN), F32),
            pltpu.VMEM((2 * side_chunks, CH, LN), F32),
            pltpu.SMEM((4 * side_chunks,), F32),
        ],
        limit=7 * MB,
    )(*sides, vec, geo, acc, ints, floats)
    side_ev, side_od = in_vmem(side_ev), in_vmem(side_od)
    image_sides = exchange(*image_sides)
    acc, known = call(
        again_kernel, "again", [VM] * 8 + [SM] * 3,
        [dense, (VM, sd((members, LN), F32))], again_scratch, limit=3 * MB,
        cost=pl.CostEstimate(flops=4 * 10**9, bytes_accessed=20 * MB, transcendentals=0),
    )(*tiles, parts, geo, vec, image, ints, down, across)
    devices = lax.axis_size("region")
    second, sums = call(
        last_kernel, "last", [VM, VM, VM, SM, VM, VM, SM, SM, VM, VM, VM, VM, VM, SM],
        [dense, (VM, sd((devices, 8, LN), F32))],
        [
            pltpu.VMEM((2 * side_chunks, 2 * members, CH), BF16),
            pltpu.VMEM((members, wide), F32),
            *again_scratch,
        ],
        limit=5 * MB,
    )(*image_sides, side_geo, side_ints, side_ev, side_od, side_down, side_across,
      acc, known, vec, image, geo, ints)
    sums = lax.all_to_all(sums, "region", 0, 0)
    field = (HB, sd((blocks, members, CH), F32))
    return tuple(call(
        update_kernel, "update", [VM, VM, VM, VM, SM, SM], [field, field],
        [
            pltpu.VMEM((blocks, members, CH), F32),
            pltpu.VMEM((blocks, members, CH), F32),
            pltpu.SemaphoreType.DMA((2, blocks)),
        ],
        limit=6 * MB,
    )(sums, vec, image, second, ints, obs_count))


def solution(mesh):
    return jax.shard_map(
        body,
        mesh=mesh,
        in_specs=(
            P(("groups", "region"), None, None),
            P(("groups", "region"), None),
            P(("groups", "region"), None),
            P(("groups", "region"), None, None),
            P(("groups", "region")),
            P(None, ("groups", "region")),
            P(("groups", "region")),
        ),
        out_specs=(P(("groups", "region"), None, None), P(("groups", "region"), None, None)),
        check_vma=False,
    )
```

```python
import functools

import jax
import jax.numpy as jnp
from jax import lax
from jax.experimental import pallas as pl
from jax.experimental.pallas import tpu as pltpu
from jax.sharding import PartitionSpec as P

REACH = 5
CUTOFF_KM = 1500.0
SCALE_KM = 1000.0
LOG2E = 1.4426950408889634
UNIT = 1.0 / CUTOFF_KM
DECAY = -LOG2E * CUTOFF_KM / SCALE_KM
LIMIT = 1.0
CH = 256
LN = 128
GROUP = 4
BATCH = 8
SPAN = 7
TINY = 1e-30
F32, BF16, I32 = jnp.float32, jnp.bfloat16, jnp.int32
VM = pl.BlockSpec(memory_space=pltpu.VMEM)
SM = pl.BlockSpec(memory_space=pltpu.SMEM)
HB = pl.BlockSpec(memory_space=pltpu.HBM)
MB = 1 << 20
OWN_HELD = 56
SIDE_HELD = 24


def lanes(shape):
    return lax.broadcasted_iota(I32, shape, len(shape) - 1)


def at(start, size=CH):
    return pl.ds(pl.multiple_of(start, LN), size)


def pack_block(rows, count, offset, dst):
    base = (offset // LN) * LN
    shift = offset - base
    lane = lanes((rows.shape[0], LN))
    low = pltpu.roll(jnp.where(lane < count, rows[:, :LN], 0.0), shift, 1)
    high = pltpu.roll(jnp.where(lane + LN < count, rows[:, LN:], 0.0), shift, 1)
    before = lane < shift
    dst[:, at(base, LN)] = jnp.where(before, dst[:, at(base, LN)], low)
    dst[:, at(base + LN, LN)] = jnp.where(before, low, high)
    dst[:, at(base + 2 * LN, LN)] = jnp.where(before, high, 0.0)
    dst[:, at(base + 3 * LN, LN)] = jnp.zeros_like(low)


def split(values):
    high = values.astype(BF16)
    return high, (values - high.astype(F32)).astype(BF16)


def put_split(values, dst, place):
    high, low = split(values)
    half = values.shape[0]
    dst[place, :half, :] = high
    dst[place, half:, :] = low


def columns(row):
    parts = [jnp.broadcast_to(row[:, k : k + LN], (LN, LN)).T for k in (0, LN)]
    return jnp.concatenate(parts, axis=0)


def build(col_x, col_y, place, row_x, row_y, tile_ref, slot):
    strip = 32
    for top in range(0, CH, strip):
        for left in range(0, CH, LN):
            dx = col_x[place, top : top + strip, :] - row_x[:, left : left + LN]
            dy = col_y[place, top : top + strip, :] - row_y[:, left : left + LN]
            square = jnp.maximum(dx * dx + dy * dy, TINY)
            distance = square * lax.rsqrt(square)
            tapered = jnp.maximum(1.0 - distance, 0.0)
            value = jnp.exp2(distance * DECAY) * (tapered * tapered)
            high, low = split(value)
            tile_ref[slot, top : top + strip, left : left + LN] = high
            tile_ref[slot, CH + top : CH + top + strip, left : left + LN] = low


def product(parts_ref, place, tile_ref, slot, transposed):
    dims = (((1,), (1 if transposed else 0,)), ((), ()))
    both = parts_ref[place]
    half = both.shape[0] // 2
    wide = lax.dot_general(both, tile_ref[slot, :CH, :], dims, preferred_element_type=F32)
    fine = lax.dot_general(both[:half], tile_ref[slot, CH:, :], dims, preferred_element_type=F32)
    return wide[:half] + wide[half:] + fine


def counted(value, t, total, sure):
    return value if sure else (t < total).astype(F32) * value


def own_product(t, total, down, across, parts_ref, tile_ref, slot, acc, sure=False):
    i, j = down[t], across[t]
    forward = product(parts_ref, i, tile_ref, slot, False)
    backward = product(parts_ref, j, tile_ref, slot, True)
    acc[:, at(j * CH)] += counted(forward, t, total, sure)
    acc[:, at(i * CH)] += counted(backward, t, total, sure)


def diagonal_product(t, total, parts_ref, tile_ref, slot, acc, sure=False):
    i = jnp.minimum(t, total - 1)
    acc[:, at(i * CH)] += counted(product(parts_ref, i, tile_ref, slot, False), t, total, sure)


def edge_product(t, total, down, across, parts_ref, tile_ref, slot, acc, sure=False):
    value = product(parts_ref, down[t], tile_ref, slot, False)
    acc[:, at(across[t] * CH)] += counted(value, t, total, sure)


def sweep(total, held, make, multiply):
    pairs = (total + 1) // 2
    full = jnp.minimum(total, 2 * held) // BATCH

    def many(p, carry):
        for half in (make, functools.partial(multiply, sure=True)):
            for u in range(BATCH):
                if half is not None:
                    half(BATCH * p + u, u % 2, BATCH // 2 * p + u // 2)
        return carry

    def few(p, carry):
        for half in (make, multiply):
            for u in range(2):
                if half is not None:
                    half(2 * p + u, u, jnp.minimum(p, held))
        return carry

    lax.fori_loop(0, full, many, 0)
    end = pairs if make is not None else jnp.minimum(pairs, held)
    lax.fori_loop(full * (BATCH // 2), end, few, 0)


def sweep_rest(total, held, make, multiply):
    def few(p, carry):
        for half in (make, multiply):
            for u in range(2):
                half(2 * p + u, u, 0)
        return carry

    lax.fori_loop(held, (total + 1) // 2, few, 0)


def remake(t, down, across, down_geo, geo, col_x, col_y, ref):
    where = at(down[t] * CH)
    col_x[0] = columns(down_geo[0:1, where])
    col_y[0] = columns(down_geo[1:2, where])
    where = at(across[t] * CH)
    build(col_x, col_y, 0, geo[0:1, where], geo[1:2, where], ref, 0)


def prepare_kernel(innov_in, pos_in, sigma_in, err_in, count_in, first_out, second_out, vec, geo,
                   parts, col_x, col_y, ints, floats, down, across, innov, pos, sigma, err, count,
                   sems):
    blocks, members = innov.shape[0], innov.shape[1]
    even = 1 - lax.rem(lax.axis_index("region"), 2)
    starts = ((1 - even) * (blocks - REACH), even * (blocks - REACH))
    ends = tuple(zip(starts, (first_out, second_out)))
    small = [(pos_in, pos), (sigma_in, sigma), (err_in, err), (count_in, count)]
    large = [(innov_in, innov)]
    for start, dst in ends:
        large.append((innov_in.at[pl.ds(start, REACH)], dst.at[:, pl.ds(0, members), :]))
    copies = [
        pltpu.make_async_copy(src, dst, sems.at[k]) for k, (src, dst) in enumerate(small + large)
    ]
    for copy in copies:
        copy.start()
    for copy in copies[: len(small)]:
        copy.wait()
    for start, dst in ends:
        for b in range(REACH):
            number = jnp.full((1, CH), count[start + b].astype(F32))
            rest = jnp.zeros((4, CH), F32)
            dst[b, members:, :] = jnp.concatenate(
                [pos[start + b], sigma[pl.ds(start + b, 1), :], number, rest], axis=0
            )
    origin = pos[0, 0:1, 0:1]
    floats[0] = jnp.max(origin)

    def pack_geo(b, offset):
        ints[b] = offset
        pair = pos[b]
        rows = jnp.concatenate(
            [
                (pair[0:1] - origin) * UNIT,
                pair[1:2] * UNIT,
                sigma[pl.ds(b, 1), :],
                err[pl.ds(b, 1), :],
                jnp.zeros((4, CH), F32),
            ],
            axis=0,
        )
        pack_block(rows, count[b], offset, geo)
        return offset + count[b]

    size = lax.fori_loop(0, blocks, pack_geo, jnp.int32(0), unroll=4)
    ints[blocks] = size
    chunks = (size + CH - 1) // CH
    for copy in copies[len(small) :]:
        copy.wait()

    def pack_vec(b, carry):
        pack_block(innov[b], count[b], ints[b], vec)
        return carry

    lax.fori_loop(0, blocks, pack_vec, 0, unroll=4)

    def prepare(p, carry):
        for u in range(GROUP):
            i = p * GROUP + u
            where = at(i * CH)
            x = geo[0:1, where]
            col_x[i] = columns(x)
            col_y[i] = columns(geo[1:2, where])
            put_split(vec[:, where] * geo[2:3, where], parts, i)
            live = lanes((1, CH)) + i * CH < size
            floats[1 + i] = jnp.min(jnp.where(live, x, 3e38))
            floats[1 + blocks + i] = jnp.max(jnp.where(live, x, -3e38))
        return carry

    lax.fori_loop(0, (chunks + GROUP - 1) // GROUP, prepare, 0)

    def enlist(i, t):
        end = floats[1 + blocks + i]
        for d in range(1, SPAN):
            j = i + d
            start = floats[1 + jnp.minimum(j, blocks - 1)]
            down[t] = i
            across[t] = j
            t = t + jnp.where((j < chunks) & (start - end < LIMIT), 1, 0)
        return t

    total = lax.fori_loop(0, chunks, enlist, jnp.int32(0))
    down[total] = 0
    across[total] = 0
    ints[blocks + 1] = total


def own_kernel(geo, parts, col_x, col_y, ints, down, across, diagonal_ev, diagonal_od, ev, od, acc):
    blocks = parts.shape[0]
    chunks = (ints[blocks] + CH - 1) // CH
    total = ints[blocks + 1]
    acc[...] = jnp.zeros_like(acc)

    def build_at(i, j, ref, slot):
        where = at(j * CH)
        build(col_x, col_y, i, geo[0:1, where], geo[1:2, where], ref, slot)

    def make_diagonal(t, which, slot):
        i = jnp.minimum(t, chunks - 1)
        build_at(i, i, (diagonal_ev, diagonal_od)[which], slot)

    def multiply_diagonal(t, which, slot, sure=False):
        diagonal_product(t, chunks, parts, (diagonal_ev, diagonal_od)[which], slot, acc, sure)

    sweep(chunks, blocks // 2, make_diagonal, multiply_diagonal)

    def make(t, which, slot):
        build_at(down[t], across[t], (ev, od)[which], slot)

    def multiply(t, which, slot, sure=False):
        own_product(t, total, down, across, parts, (ev, od)[which], slot, acc, sure)

    sweep(total, ev.shape[0] - 1, make, multiply)


def edge_kernel(from_first, from_second, vec, geo, acc, ints, floats, ev, od, side_geo, side_ints,
                down, across, out, parts, first_out, second_out, side_vec, side_parts, col_x, col_y,
                floats_side):
    members = vec.shape[0]
    blocks = (vec.shape[1] - 2 * CH) // CH
    wide = side_vec.shape[1] // 2
    size = ints[blocks]
    chunks = (size + CH - 1) // CH
    origin = floats[0]
    out[...] = jnp.zeros_like(out)
    side_ends = []
    even = 1 - lax.rem(lax.axis_index("region"), 2)
    for side, ref in enumerate((from_first, from_second)):
        offset = jnp.int32(side * wide)
        for b in range(REACH):
            misc = ref[b, members:, :]
            number = misc[3, 0].astype(I32)
            pack_block(ref[b, :members, :], number, offset, side_vec)
            rows = jnp.concatenate(
                [(misc[0:1] - origin) * UNIT, misc[1:2] * UNIT, misc[2:]], axis=0
            )
            pack_block(rows, number, offset, side_geo)
            offset = offset + number
        side_ends.append(offset)
    down[0] = 0
    across[0] = 0
    side_chunks = [(end - k * wide + CH - 1) // CH for k, end in enumerate(side_ends)]

    def prepare(p, t):
        for h, side in ((2 * p, 0), (2 * p, 1), (2 * p + 1, 0), (2 * p + 1, 1)):
            place = side * (wide // CH) + h
            where = at(place * CH)
            x = side_geo[0:1, where]
            col_x[place] = columns(x)
            col_y[place] = columns(side_geo[1:2, where])
            put_split(side_vec[:, where] * side_geo[2:3, where], side_parts, place)
            live = lanes((1, CH)) + place * CH < side_ends[side]
            floats_side[2 * place] = jnp.min(jnp.where(live, x, 3e38))
            floats_side[2 * place + 1] = jnp.max(jnp.where(live, x, -3e38))
        return t

    lax.fori_loop(0, (jnp.maximum(*side_chunks) + 1) // 2, prepare, 0)
    total = jnp.int32(0)
    for side in range(2):
        ahead = even == side

        def enlist(h, t, side=side, ahead=ahead):
            place = side * (wide // CH) + h
            low, high = floats_side[2 * place], floats_side[2 * place + 1]
            for d in range(SPAN):
                i = jnp.where(ahead, jnp.maximum(chunks - 1 - d, 0), jnp.minimum(d, chunks - 1))
                apart = jnp.where(ahead, low - floats[1 + blocks + i], floats[1 + i] - high)
                down[t] = place
                across[t] = i
                t = t + jnp.where((apart < LIMIT) & (d < chunks), 1, 0)
            return t

        total = lax.fori_loop(0, side_chunks[side], enlist, total)
    last = jnp.maximum(total - 1, 0)
    down[total] = down[last]
    across[total] = across[last]
    side_ints[0] = total
    for side in range(2):
        side_ints[1 + side] = side_chunks[side]

    def make(t, which, slot):
        where = at(across[t] * CH)
        build(col_x, col_y, down[t], geo[0:1, where], geo[1:2, where], (ev, od)[which], slot)

    def multiply(t, which, slot, sure=False):
        edge_product(t, total, down, across, side_parts, (ev, od)[which], slot, out, sure)

    sweep(total, ev.shape[0] - 1, make, multiply)

    def finish(i, carry):
        where = at(i * CH)
        scale = geo[2:3, where]
        image = scale * (out[:, where] + acc[:, where]) + geo[3:4, where] * vec[:, where]
        out[:, where] = image
        put_split(image * scale, parts, i)
        return carry

    lax.fori_loop(0, chunks, finish, 0)
    tail = ints[blocks - REACH]
    for start, dst in (((1 - even) * tail, first_out), (even * tail, second_out)):
        base = (start // LN) * LN
        shift = start - base
        back = lax.rem(LN - shift, LN)
        keep = lanes((members, LN)) < LN - shift
        turned = pltpu.roll(out[:, at(base, LN)], back, 1)
        for k in range(REACH * CH // LN):
            following = pltpu.roll(out[:, at(base + (k + 1) * LN, LN)], back, 1)
            dst[:, k * LN : (k + 1) * LN] = jnp.where(keep, turned, following)
            turned = following


def halves(values):
    return values[:, :LN] + values[:, LN:]


def lane_sum(values):
    return jnp.sum(values, axis=1, keepdims=True)


def again_kernel(diagonal_ev, diagonal_od, ev, od, parts, geo, vec, image, ints, down, across, acc,
                 known, col_x, col_y, ev_more, od_more):
    blocks = acc.shape[1] // CH - 2
    total = ints[blocks + 1]
    held = ev.shape[0] - 1
    acc[...] = jnp.zeros_like(acc)
    more = (ev_more, od_more)
    chunks = (ints[blocks] + CH - 1) // CH

    def multiply_diagonal(t, which, slot, sure=False):
        diagonal_product(t, chunks, parts, (diagonal_ev, diagonal_od)[which], slot, acc, sure)

    sweep(chunks, blocks // 2, None, multiply_diagonal)

    def multiply(t, which, slot, sure=False):
        own_product(t, total, down, across, parts, (ev, od)[which], slot, acc, sure)

    sweep(total, held, None, multiply)

    def make_more(t, which, slot):
        remake(t, down, across, geo, geo, col_x, col_y, more[which])

    def multiply_more(t, which, slot):
        own_product(t, total, down, across, parts, more[which], slot, acc)

    sweep_rest(total, held, make_more, multiply_more)
    members = vec.shape[0]
    zero = jnp.zeros((members, LN), F32)

    def first(i, carry):
        m0, m1 = carry
        r, y = vec[:, at(i * CH)], image[:, at(i * CH)]
        return m0 + halves(r * r), m1 + halves(r * y)

    m0, m1 = (lane_sum(x) for x in lax.fori_loop(0, chunks, first, (zero, zero)))
    mean = jnp.where(m0 > 0, m1 / jnp.where(m0 > 0, m0, 1.0), 0.0)

    def second(i, carry):
        vv, cross, slip = carry
        r, y = vec[:, at(i * CH)], image[:, at(i * CH)]
        z = y - mean * r
        return vv + halves(z * z), cross + halves(z * y), slip + halves(z * r)

    vv, cross, slip = (lane_sum(x) for x in lax.fori_loop(0, chunks, second, (zero, zero, zero)))
    table = jnp.zeros((members, LN), F32)
    lane = lanes((members, LN))
    for k, value in ((0, m0), (1, m1), (2, mean), (3, vv), (5, cross), (6, slip)):
        table = jnp.where(lane == k, value, table)
    known[...] = table


def last_kernel(from_first, from_second, side_geo, side_ints, ev, od, down, across, acc, known, vec,
                image, geo, ints, out, sums, side_parts, total_ref, col_x, col_y, ev_more, od_more):
    members = vec.shape[0]
    blocks = vec.shape[1] // CH - 2
    chunks = (ints[blocks] + CH - 1) // CH
    total = side_ints[0]
    per_side = side_geo.shape[1] // CH // 2

    def carry_over(i, carry):
        total_ref[:, at(i * CH)] = acc[:, at(i * CH)]
        return carry

    lax.fori_loop(0, chunks, carry_over, 0)
    for side, ref in enumerate((from_first, from_second)):

        def scale_side(h, carry, side=side, ref=ref):
            place = side * per_side + h
            scale = side_geo[2:3, at(place * CH)]
            put_split(ref[:, at(h * CH)] * scale, side_parts, place)
            return carry

        lax.fori_loop(0, side_ints[1 + side], scale_side, 0)
    held = ev.shape[0] - 1
    more = (ev_more, od_more)

    def multiply(t, which, slot, sure=False):
        edge_product(t, total, down, across, side_parts, (ev, od)[which], slot, total_ref, sure)

    sweep(total, held, None, multiply)

    def make_more(t, which, slot):
        remake(t, down, across, side_geo, geo, col_x, col_y, more[which])

    def multiply_more(t, which, slot):
        edge_product(t, total, down, across, side_parts, more[which], slot, total_ref)

    sweep_rest(total, held, make_more, multiply_more)
    zero = jnp.zeros((members, LN), F32)
    mean = known[:, 2:3]
    tail = jnp.zeros((members, 2 * LN), F32)
    for k in range(2):
        out[:, at((chunks + k) * CH)] = tail

    def sums_of(i, carry):
        zu, cross = carry
        where = at(i * CH)
        r, y = vec[:, where], image[:, where]
        yy = geo[2:3, where] * total_ref[:, where] + geo[3:4, where] * y
        out[:, where] = yy
        u = yy - mean * y
        return zu + halves((y - mean * r) * u), cross + halves(r * u)

    zu, cross = (lane_sum(x) for x in lax.fori_loop(0, chunks, sums_of, (zero, zero)))
    lane = lanes((members, LN))
    table = known[...]
    table = jnp.where(lane == 4, zu, table)
    table = jnp.where(lane == 5, cross + table, table)
    turned = jnp.concatenate([table, jnp.zeros((LN - members, LN), F32)], axis=0).T[:8]
    for k in range(sums.shape[0]):
        sums[k] = turned


def update_kernel(sums, vec, image, second, ints, count, solution_out, residual_out, solution_ref,
                  residual_ref, sems):
    members = vec.shape[0]
    blocks = vec.shape[1] // CH - 2
    chunks = (ints[blocks] + CH - 1) // CH
    terms = sums[...]
    m0 = jnp.sum(terms[:, 0, :], axis=0, keepdims=True)
    m1 = jnp.sum(terms[:, 1, :], axis=0, keepdims=True)
    used = lanes((1, LN)) < members
    m0 = jnp.where(used, m0, 1.0)
    m1 = jnp.where(used, m1, 1.0)
    mean = m1 / m0
    off = mean - terms[:, 2, :]
    vv = terms[:, 3, :] - 2.0 * off * terms[:, 6, :] + off * off * terms[:, 0, :]
    zu = terms[:, 4, :] - off * terms[:, 5, :] + off * off * terms[:, 1, :]
    cross = terms[:, 5, :] - 2.0 * off * terms[:, 1, :]
    vv, zu, cross = (jnp.sum(x, axis=0, keepdims=True) for x in (vv, zu, cross))
    alpha = m0 / m1
    rr = alpha * alpha * vv
    beta = rr / m0
    alpha_next = rr / (alpha * alpha * zu - alpha * beta * cross + beta * beta * m1)
    one = alpha + alpha_next * (1.0 + beta)
    two = alpha * alpha_next
    table = jnp.concatenate([one, two, jnp.zeros((LN - 2, LN), F32)], axis=0).T
    one, two = table[:members, 0:1], table[:members, 1:2]

    copies = []
    lane = lanes((2 * members, LN))
    for b in range(blocks):
        offset, number = ints[b], count[b]
        base = (offset // LN) * LN
        shift = offset - base
        back = lax.rem(LN - shift, LN)
        keep = lane < LN - shift
        turned = []
        for k in range(3):
            where = at(base + k * LN, LN)
            r, y, yy = vec[:, where], image[:, where], second[:, where]
            both = jnp.concatenate([one * r - two * y, r - one * y + two * yy], axis=0)
            turned.append(pltpu.roll(both, back, 1))
        for k in range(2):
            part = jnp.where(keep, turned[k], turned[k + 1])
            part = jnp.where(lane + k * LN < number, part, 0.0)
            solution_ref[b, :, k * LN : (k + 1) * LN] = part[:members]
            residual_ref[b, :, k * LN : (k + 1) * LN] = part[members:]
        for k, (src, dst) in enumerate(((solution_ref, solution_out), (residual_ref, residual_out))):
            copy = pltpu.make_async_copy(src.at[b], dst.at[b], sems.at[k, b])
            copy.start()
            copies.append(copy)
    for copy in copies:
        copy.wait()


def exchange(first, second):
    devices = lax.axis_size("region")
    received = []
    for start, block in ((1, first), (0, second)):
        pairs = [(i, i + 1) for i in range(start, devices - 1, 2)]
        received.append(lax.ppermute(block, "region", pairs + [(b, a) for a, b in pairs]))
    return received


def call(kernel, name, in_specs, outs, scratch=(), limit=9 * MB, cost=None):
    return pl.pallas_call(
        kernel,
        name=name,
        in_specs=in_specs,
        out_specs=[spec for spec, _ in outs],
        out_shape=[shape for _, shape in outs],
        scratch_shapes=list(scratch),
        compiler_params=pltpu.CompilerParams(vmem_limit_bytes=limit),
        cost_estimate=cost,
    )


def body(obs_pos, obs_sigma, obs_error, innovation, obs_count, pair_list, pair_live):
    blocks, members, _ = innovation.shape
    sd = jax.ShapeDtypeStruct
    in_hbm = functools.partial(pltpu.with_memory_space_constraint, memory_space=pltpu.HBM)
    in_vmem = functools.partial(pltpu.with_memory_space_constraint, memory_space=pltpu.VMEM)
    wide = blocks * CH + 2 * CH
    side_chunks = REACH + 2
    own_slots = [blocks // 2 + 1] * 2 + [OWN_HELD // 2 + 1] * 2
    side_slots = SIDE_HELD // 2 + 1
    listed = blocks * SPAN + 16
    pack_out = (VM, sd((REACH, members + 8, CH), F32))
    again_scratch = [
        pltpu.VMEM((1, CH, LN), F32),
        pltpu.VMEM((1, CH, LN), F32),
        pltpu.VMEM((1, 2 * CH, CH), BF16),
        pltpu.VMEM((1, 2 * CH, CH), BF16),
    ]
    dense = (VM, sd((members, wide), F32))
    tile = (2 * CH, CH)
    column = (VM, sd((blocks, CH, LN), F32))
    *sides, vec, geo, parts, col_x, col_y, ints, floats, down, across = call(
        prepare_kernel, "prepare", [HB] * 5,
        [
            pack_out,
            pack_out,
            dense,
            (VM, sd((8, wide), F32)),
            (VM, sd((blocks, 2 * members, CH), BF16)),
            column,
            column,
            (SM, sd((blocks + 2,), I32)),
            (SM, sd((2 * blocks + 1,), F32)),
            (SM, sd((listed,), I32)),
            (SM, sd((listed,), I32)),
        ],
        [
            pltpu.VMEM(innovation.shape, F32),
            pltpu.VMEM(obs_pos.shape, F32),
            pltpu.VMEM(obs_sigma.shape, F32),
            pltpu.VMEM(obs_error.shape, F32),
            pltpu.SMEM(obs_count.shape, I32),
            pltpu.SemaphoreType.DMA((7,)),
        ],
        limit=9 * MB,
    )(*map(in_hbm, (innovation, obs_pos, obs_sigma, obs_error, obs_count)))
    sides = exchange(*sides)
    *tiles, acc = call(
        own_kernel, "own", [VM, VM, VM, VM, SM, SM, SM],
        [(VM, pltpu.VMEM((slots,) + tile, BF16)) for slots in own_slots] + [dense],
        limit=6 * MB,
        cost=pl.CostEstimate(flops=4 * 10**9, bytes_accessed=20 * MB, transcendentals=0),
    )(geo, parts, col_x, col_y, ints, down, across)
    tiles = map(in_vmem, tiles)
    side = (VM, sd((members, REACH * CH), F32))
    (side_ev, side_od, side_geo, side_ints, side_down, side_across, image, parts,
     *image_sides) = call(
        edge_kernel, "edge", [VM, VM, VM, VM, VM, SM, SM],
        [
            (VM, pltpu.VMEM((side_slots,) + tile, BF16)),
            (VM, pltpu.VMEM((side_slots,) + tile, BF16)),
            (VM, sd((8, 2 * side_chunks * CH), F32)),
            (SM, sd((3,), I32)),
            (SM, sd((128,), I32)),
            (SM, sd((128,), I32)),
            dense,
            (VM, sd((blocks, 2 * members, CH), BF16)),
            side,
            side,
        ],
        [
            pltpu.VMEM((members, 2 * side_chunks * CH), F32),
            pltpu.VMEM((2 * side_chunks, 2 * members, CH), BF16),
            pltpu.VMEM((2 * side_chunks, CH, LN), F32),
            pltpu.VMEM((2 * side_chunks, CH, LN), F32),
            pltpu.SMEM((4 * side_chunks,), F32),
        ],
        limit=7 * MB,
    )(*sides, vec, geo, acc, ints, floats)
    side_ev, side_od = in_vmem(side_ev), in_vmem(side_od)
    image_sides = exchange(*image_sides)
    acc, known = call(
        again_kernel, "again", [VM] * 8 + [SM] * 3,
        [dense, (VM, sd((members, LN), F32))], again_scratch, limit=3 * MB,
        cost=pl.CostEstimate(flops=4 * 10**9, bytes_accessed=20 * MB, transcendentals=0),
    )(*tiles, parts, geo, vec, image, ints, down, across)
    devices = lax.axis_size("region")
    second, sums = call(
        last_kernel, "last", [VM, VM, VM, SM, VM, VM, SM, SM, VM, VM, VM, VM, VM, SM],
        [dense, (VM, sd((devices, 8, LN), F32))],
        [
            pltpu.VMEM((2 * side_chunks, 2 * members, CH), BF16),
            pltpu.VMEM((members, wide), F32),
            *again_scratch,
        ],
        limit=5 * MB,
    )(*image_sides, side_geo, side_ints, side_ev, side_od, side_down, side_across,
      acc, known, vec, image, geo, ints)
    sums = lax.all_to_all(sums, "region", 0, 0)
    field = (HB, sd((blocks, members, CH), F32))
    return tuple(call(
        update_kernel, "update", [VM, VM, VM, VM, SM, SM], [field, field],
        [
            pltpu.VMEM((blocks, members, CH), F32),
            pltpu.VMEM((blocks, members, CH), F32),
            pltpu.SemaphoreType.DMA((2, blocks)),
        ],
        limit=6 * MB,
    )(sums, vec, image, second, ints, obs_count))


def solution(mesh):
    return jax.shard_map(
        body,
        mesh=mesh,
        in_specs=(
            P(("groups", "region"), None, None),
            P(("groups", "region"), None),
            P(("groups", "region"), None),
            P(("groups", "region"), None, None),
            P(("groups", "region")),
            P(None, ("groups", "region")),
            P(("groups", "region")),
        ),
        out_specs=(P(("groups", "region"), None, None), P(("groups", "region"), None, None)),
        check_vma=False,
    )
```

```python
import functools

import jax
import jax.numpy as jnp
from jax import lax
from jax.experimental import pallas as pl
from jax.experimental.pallas import tpu as pltpu
from jax.sharding import PartitionSpec as P

REACH = 5
CUTOFF_KM = 1500.0
SCALE_KM = 1000.0
LOG2E = 1.4426950408889634
UNIT = 1.0 / CUTOFF_KM
DECAY = -LOG2E * CUTOFF_KM / SCALE_KM
LIMIT = 1.0
CH = 256
LN = 128
GROUP = 4
BATCH = 8
SPAN = 7
TINY = 1e-30
F32, BF16, I32 = jnp.float32, jnp.bfloat16, jnp.int32
VM = pl.BlockSpec(memory_space=pltpu.VMEM)
SM = pl.BlockSpec(memory_space=pltpu.SMEM)
HB = pl.BlockSpec(memory_space=pltpu.HBM)
MB = 1 << 20
OWN_HELD = 56
SIDE_HELD = 24


def lanes(shape):
    return lax.broadcasted_iota(I32, shape, len(shape) - 1)


def at(start, size=CH):
    return pl.ds(pl.multiple_of(start, LN), size)


def pack_block(rows, count, offset, dst):
    base = (offset // LN) * LN
    shift = offset - base
    lane = lanes((rows.shape[0], LN))
    low = pltpu.roll(jnp.where(lane < count, rows[:, :LN], 0.0), shift, 1)
    high = pltpu.roll(jnp.where(lane + LN < count, rows[:, LN:], 0.0), shift, 1)
    before = lane < shift
    dst[:, at(base, LN)] = jnp.where(before, dst[:, at(base, LN)], low)
    dst[:, at(base + LN, LN)] = jnp.where(before, low, high)
    dst[:, at(base + 2 * LN, LN)] = jnp.where(before, high, 0.0)
    dst[:, at(base + 3 * LN, LN)] = jnp.zeros_like(low)


def split(values):
    high = values.astype(BF16)
    return high, (values - high.astype(F32)).astype(BF16)


def put_split(values, dst, place):
    high, low = split(values)
    half = values.shape[0]
    dst[place, :half, :] = high
    dst[place, half:, :] = low


def columns(row):
    parts = [jnp.broadcast_to(row[:, k : k + LN], (LN, LN)).T for k in (0, LN)]
    return jnp.concatenate(parts, axis=0)


def build(col_x, col_y, place, row_x, row_y, tile_ref, slot):
    strip = 32
    for top in range(0, CH, strip):
        for left in range(0, CH, LN):
            dx = col_x[place, top : top + strip, :] - row_x[:, left : left + LN]
            dy = col_y[place, top : top + strip, :] - row_y[:, left : left + LN]
            square = jnp.maximum(dx * dx + dy * dy, TINY)
            distance = square * lax.rsqrt(square)
            tapered = jnp.maximum(1.0 - distance, 0.0)
            value = jnp.exp2(distance * DECAY) * (tapered * tapered)
            high, low = split(value)
            tile_ref[slot, top : top + strip, left : left + LN] = high
            tile_ref[slot, CH + top : CH + top + strip, left : left + LN] = low


def product(parts_ref, place, tile_ref, slot, transposed):
    dims = (((1,), (1 if transposed else 0,)), ((), ()))
    both = parts_ref[place]
    half = both.shape[0] // 2
    wide = lax.dot_general(both, tile_ref[slot, :CH, :], dims, preferred_element_type=F32)
    fine = lax.dot_general(both[:half], tile_ref[slot, CH:, :], dims, preferred_element_type=F32)
    return wide[:half] + wide[half:] + fine


def counted(value, t, total, sure):
    return value if sure else (t < total).astype(F32) * value


def own_product(t, total, down, across, parts_ref, tile_ref, slot, acc, sure=False):
    i, j = down[t], across[t]
    forward = product(parts_ref, i, tile_ref, slot, False)
    backward = product(parts_ref, j, tile_ref, slot, True)
    acc[:, at(j * CH)] += counted(forward, t, total, sure)
    acc[:, at(i * CH)] += counted(backward, t, total, sure)


def diagonal_product(t, total, parts_ref, tile_ref, slot, acc, sure=False):
    i = jnp.minimum(t, total - 1)
    acc[:, at(i * CH)] += counted(product(parts_ref, i, tile_ref, slot, False), t, total, sure)


def edge_product(t, total, down, across, parts_ref, tile_ref, slot, acc, sure=False):
    value = product(parts_ref, down[t], tile_ref, slot, False)
    acc[:, at(across[t] * CH)] += counted(value, t, total, sure)


def sweep(total, held, make, multiply):
    pairs = (total + 1) // 2
    full = jnp.minimum(total, 2 * held) // BATCH

    def many(p, carry):
        for half in (make, functools.partial(multiply, sure=True)):
            for u in range(BATCH):
                if half is not None:
                    half(BATCH * p + u, u % 2, BATCH // 2 * p + u // 2)
        return carry

    def few(p, carry):
        for half in (make, multiply):
            for u in range(2):
                if half is not None:
                    half(2 * p + u, u, jnp.minimum(p, held))
        return carry

    lax.fori_loop(0, full, many, 0)
    end = pairs if make is not None else jnp.minimum(pairs, held)
    lax.fori_loop(full * (BATCH // 2), end, few, 0)


def sweep_rest(total, held, make, multiply):
    def few(p, carry):
        for half in (make, multiply):
            for u in range(2):
                half(2 * p + u, u, 0)
        return carry

    lax.fori_loop(held, (total + 1) // 2, few, 0)


def remake(t, down, across, down_geo, geo, col_x, col_y, ref):
    where = at(down[t] * CH)
    col_x[0] = columns(down_geo[0:1, where])
    col_y[0] = columns(down_geo[1:2, where])
    where = at(across[t] * CH)
    build(col_x, col_y, 0, geo[0:1, where], geo[1:2, where], ref, 0)


def prepare_kernel(innov_in, pos_in, sigma_in, err_in, count_in, first_out, second_out, vec, geo,
                   parts, col_x, col_y, ints, floats, down, across, innov, pos, sigma, err, count,
                   sems):
    blocks, members = innov.shape[0], innov.shape[1]
    even = 1 - lax.rem(lax.axis_index("region"), 2)
    starts = ((1 - even) * (blocks - REACH), even * (blocks - REACH))
    ends = tuple(zip(starts, (first_out, second_out)))
    small = [(pos_in, pos), (sigma_in, sigma), (err_in, err), (count_in, count)]
    large = [(innov_in, innov)]
    for start, dst in ends:
        large.append((innov_in.at[pl.ds(start, REACH)], dst.at[:, pl.ds(0, members), :]))
    copies = [
        pltpu.make_async_copy(src, dst, sems.at[k]) for k, (src, dst) in enumerate(small + large)
    ]
    for copy in copies:
        copy.start()
    for copy in copies[: len(small)]:
        copy.wait()
    for start, dst in ends:
        for b in range(REACH):
            number = jnp.full((1, CH), count[start + b].astype(F32))
            rest = jnp.zeros((4, CH), F32)
            dst[b, members:, :] = jnp.concatenate(
                [pos[start + b], sigma[pl.ds(start + b, 1), :], number, rest], axis=0
            )
    origin = pos[0, 0:1, 0:1]
    floats[0] = jnp.max(origin)

    def pack_geo(b, offset):
        ints[b] = offset
        pair = pos[b]
        rows = jnp.concatenate(
            [
                (pair[0:1] - origin) * UNIT,
                pair[1:2] * UNIT,
                sigma[pl.ds(b, 1), :],
                err[pl.ds(b, 1), :],
                jnp.zeros((4, CH), F32),
            ],
            axis=0,
        )
        pack_block(rows, count[b], offset, geo)
        return offset + count[b]

    size = lax.fori_loop(0, blocks, pack_geo, jnp.int32(0), unroll=16)
    ints[blocks] = size
    chunks = (size + CH - 1) // CH
    for copy in copies[len(small) :]:
        copy.wait()

    def pack_vec(b, carry):
        pack_block(innov[b], count[b], ints[b], vec)
        return carry

    lax.fori_loop(0, blocks, pack_vec, 0, unroll=16)

    def prepare(p, carry):
        for u in range(GROUP):
            i = p * GROUP + u
            where = at(i * CH)
            x = geo[0:1, where]
            col_x[i] = columns(x)
            col_y[i] = columns(geo[1:2, where])
            put_split(vec[:, where] * geo[2:3, where], parts, i)
            live = lanes((1, CH)) + i * CH < size
            floats[1 + i] = jnp.min(jnp.where(live, x, 3e38))
            floats[1 + blocks + i] = jnp.max(jnp.where(live, x, -3e38))
        return carry

    lax.fori_loop(0, (chunks + GROUP - 1) // GROUP, prepare, 0)

    def enlist(i, t):
        end = floats[1 + blocks + i]
        for d in range(1, SPAN):
            j = i + d
            start = floats[1 + jnp.minimum(j, blocks - 1)]
            down[t] = i
            across[t] = j
            t = t + jnp.where((j < chunks) & (start - end < LIMIT), 1, 0)
        return t

    total = lax.fori_loop(0, chunks, enlist, jnp.int32(0))
    down[total] = 0
    across[total] = 0
    ints[blocks + 1] = total


def own_kernel(geo, parts, col_x, col_y, ints, down, across, diagonal_ev, diagonal_od, ev, od, acc):
    blocks = parts.shape[0]
    chunks = (ints[blocks] + CH - 1) // CH
    total = ints[blocks + 1]
    acc[...] = jnp.zeros_like(acc)

    def build_at(i, j, ref, slot):
        where = at(j * CH)
        build(col_x, col_y, i, geo[0:1, where], geo[1:2, where], ref, slot)

    def make_diagonal(t, which, slot):
        i = jnp.minimum(t, chunks - 1)
        build_at(i, i, (diagonal_ev, diagonal_od)[which], slot)

    def multiply_diagonal(t, which, slot, sure=False):
        diagonal_product(t, chunks, parts, (diagonal_ev, diagonal_od)[which], slot, acc, sure)

    sweep(chunks, blocks // 2, make_diagonal, multiply_diagonal)

    def make(t, which, slot):
        build_at(down[t], across[t], (ev, od)[which], slot)

    def multiply(t, which, slot, sure=False):
        own_product(t, total, down, across, parts, (ev, od)[which], slot, acc, sure)

    sweep(total, ev.shape[0] - 1, make, multiply)


def edge_kernel(from_first, from_second, vec, geo, acc, ints, floats, ev, od, side_geo, side_ints,
                down, across, out, parts, first_out, second_out, side_vec, side_parts, col_x, col_y,
                floats_side):
    members = vec.shape[0]
    blocks = (vec.shape[1] - 2 * CH) // CH
    wide = side_vec.shape[1] // 2
    size = ints[blocks]
    chunks = (size + CH - 1) // CH
    origin = floats[0]
    out[...] = jnp.zeros_like(out)
    side_ends = []
    even = 1 - lax.rem(lax.axis_index("region"), 2)
    for side, ref in enumerate((from_first, from_second)):
        offset = jnp.int32(side * wide)
        for b in range(REACH):
            misc = ref[b, members:, :]
            number = misc[3, 0].astype(I32)
            pack_block(ref[b, :members, :], number, offset, side_vec)
            rows = jnp.concatenate(
                [(misc[0:1] - origin) * UNIT, misc[1:2] * UNIT, misc[2:]], axis=0
            )
            pack_block(rows, number, offset, side_geo)
            offset = offset + number
        side_ends.append(offset)
    down[0] = 0
    across[0] = 0
    side_chunks = [(end - k * wide + CH - 1) // CH for k, end in enumerate(side_ends)]

    def prepare(p, t):
        for h, side in ((2 * p, 0), (2 * p, 1), (2 * p + 1, 0), (2 * p + 1, 1)):
            place = side * (wide // CH) + h
            where = at(place * CH)
            x = side_geo[0:1, where]
            col_x[place] = columns(x)
            col_y[place] = columns(side_geo[1:2, where])
            put_split(side_vec[:, where] * side_geo[2:3, where], side_parts, place)
            live = lanes((1, CH)) + place * CH < side_ends[side]
            floats_side[2 * place] = jnp.min(jnp.where(live, x, 3e38))
            floats_side[2 * place + 1] = jnp.max(jnp.where(live, x, -3e38))
        return t

    lax.fori_loop(0, (jnp.maximum(*side_chunks) + 1) // 2, prepare, 0)
    total = jnp.int32(0)
    for side in range(2):
        ahead = even == side

        def enlist(h, t, side=side, ahead=ahead):
            place = side * (wide // CH) + h
            low, high = floats_side[2 * place], floats_side[2 * place + 1]
            for d in range(SPAN):
                i = jnp.where(ahead, jnp.maximum(chunks - 1 - d, 0), jnp.minimum(d, chunks - 1))
                apart = jnp.where(ahead, low - floats[1 + blocks + i], floats[1 + i] - high)
                down[t] = place
                across[t] = i
                t = t + jnp.where((apart < LIMIT) & (d < chunks), 1, 0)
            return t

        total = lax.fori_loop(0, side_chunks[side], enlist, total)
    last = jnp.maximum(total - 1, 0)
    down[total] = down[last]
    across[total] = across[last]
    side_ints[0] = total
    for side in range(2):
        side_ints[1 + side] = side_chunks[side]

    def make(t, which, slot):
        where = at(across[t] * CH)
        build(col_x, col_y, down[t], geo[0:1, where], geo[1:2, where], (ev, od)[which], slot)

    def multiply(t, which, slot, sure=False):
        edge_product(t, total, down, across, side_parts, (ev, od)[which], slot, out, sure)

    sweep(total, ev.shape[0] - 1, make, multiply)

    def finish(i, carry):
        where = at(i * CH)
        scale = geo[2:3, where]
        image = scale * (out[:, where] + acc[:, where]) + geo[3:4, where] * vec[:, where]
        out[:, where] = image
        put_split(image * scale, parts, i)
        return carry

    lax.fori_loop(0, chunks, finish, 0)
    tail = ints[blocks - REACH]
    for start, dst in (((1 - even) * tail, first_out), (even * tail, second_out)):
        base = (start // LN) * LN
        shift = start - base
        back = lax.rem(LN - shift, LN)
        keep = lanes((members, LN)) < LN - shift
        turned = pltpu.roll(out[:, at(base, LN)], back, 1)
        for k in range(REACH * CH // LN):
            following = pltpu.roll(out[:, at(base + (k + 1) * LN, LN)], back, 1)
            dst[:, k * LN : (k + 1) * LN] = jnp.where(keep, turned, following)
            turned = following


def halves(values):
    return values[:, :LN] + values[:, LN:]


def lane_sum(values):
    return jnp.sum(values, axis=1, keepdims=True)


def again_kernel(diagonal_ev, diagonal_od, ev, od, parts, geo, vec, image, ints, down, across, acc,
                 known, col_x, col_y, ev_more, od_more):
    blocks = acc.shape[1] // CH - 2
    total = ints[blocks + 1]
    held = ev.shape[0] - 1
    acc[...] = jnp.zeros_like(acc)
    more = (ev_more, od_more)
    chunks = (ints[blocks] + CH - 1) // CH

    def multiply_diagonal(t, which, slot, sure=False):
        diagonal_product(t, chunks, parts, (diagonal_ev, diagonal_od)[which], slot, acc, sure)

    sweep(chunks, blocks // 2, None, multiply_diagonal)

    def multiply(t, which, slot, sure=False):
        own_product(t, total, down, across, parts, (ev, od)[which], slot, acc, sure)

    sweep(total, held, None, multiply)

    def make_more(t, which, slot):
        remake(t, down, across, geo, geo, col_x, col_y, more[which])

    def multiply_more(t, which, slot):
        own_product(t, total, down, across, parts, more[which], slot, acc)

    sweep_rest(total, held, make_more, multiply_more)
    members = vec.shape[0]
    zero = jnp.zeros((members, LN), F32)

    def first(i, carry):
        m0, m1 = carry
        r, y = vec[:, at(i * CH)], image[:, at(i * CH)]
        return m0 + halves(r * r), m1 + halves(r * y)

    m0, m1 = (lane_sum(x) for x in lax.fori_loop(0, chunks, first, (zero, zero)))
    mean = jnp.where(m0 > 0, m1 / jnp.where(m0 > 0, m0, 1.0), 0.0)

    def second(i, carry):
        vv, cross, slip = carry
        r, y = vec[:, at(i * CH)], image[:, at(i * CH)]
        z = y - mean * r
        return vv + halves(z * z), cross + halves(z * y), slip + halves(z * r)

    vv, cross, slip = (lane_sum(x) for x in lax.fori_loop(0, chunks, second, (zero, zero, zero)))
    table = jnp.zeros((members, LN), F32)
    lane = lanes((members, LN))
    for k, value in ((0, m0), (1, m1), (2, mean), (3, vv), (5, cross), (6, slip)):
        table = jnp.where(lane == k, value, table)
    known[...] = table


def last_kernel(from_first, from_second, side_geo, side_ints, ev, od, down, across, acc, known, vec,
                image, geo, ints, out, sums, side_parts, total_ref, col_x, col_y, ev_more, od_more):
    members = vec.shape[0]
    blocks = vec.shape[1] // CH - 2
    chunks = (ints[blocks] + CH - 1) // CH
    total = side_ints[0]
    per_side = side_geo.shape[1] // CH // 2

    def carry_over(i, carry):
        total_ref[:, at(i * CH)] = acc[:, at(i * CH)]
        return carry

    lax.fori_loop(0, chunks, carry_over, 0)

    def scale_sides(h, carry):
        for side, ref in enumerate((from_first, from_second)):
            place = side * per_side + h
            scale = side_geo[2:3, at(place * CH)]
            put_split(ref[:, at(h * CH)] * scale, side_parts, place)
        return carry

    lax.fori_loop(0, jnp.maximum(side_ints[1], side_ints[2]), scale_sides, 0)
    held = ev.shape[0] - 1
    more = (ev_more, od_more)

    def multiply(t, which, slot, sure=False):
        edge_product(t, total, down, across, side_parts, (ev, od)[which], slot, total_ref, sure)

    sweep(total, held, None, multiply)

    def make_more(t, which, slot):
        remake(t, down, across, side_geo, geo, col_x, col_y, more[which])

    def multiply_more(t, which, slot):
        edge_product(t, total, down, across, side_parts, more[which], slot, total_ref)

    sweep_rest(total, held, make_more, multiply_more)
    zero = jnp.zeros((members, LN), F32)
    mean = known[:, 2:3]
    tail = jnp.zeros((members, 2 * LN), F32)
    for k in range(2):
        out[:, at((chunks + k) * CH)] = tail

    def sums_of(i, carry):
        zu, cross = carry
        where = at(i * CH)
        r, y = vec[:, where], image[:, where]
        yy = geo[2:3, where] * total_ref[:, where] + geo[3:4, where] * y
        out[:, where] = yy
        u = yy - mean * y
        return zu + halves((y - mean * r) * u), cross + halves(r * u)

    zu, cross = (lane_sum(x) for x in lax.fori_loop(0, chunks, sums_of, (zero, zero)))
    lane = lanes((members, LN))
    table = known[...]
    table = jnp.where(lane == 4, zu, table)
    table = jnp.where(lane == 5, cross + table, table)
    turned = jnp.concatenate([table, jnp.zeros((LN - members, LN), F32)], axis=0).T[:8]
    for k in range(sums.shape[0]):
        sums[k] = turned


def update_kernel(sums, vec, image, second, ints, solution_out, residual_out, solution_ref,
                  residual_ref, sems):
    members = vec.shape[0]
    blocks = vec.shape[1] // CH - 2
    chunks = (ints[blocks] + CH - 1) // CH
    terms = sums[...]
    m0 = jnp.sum(terms[:, 0, :], axis=0, keepdims=True)
    m1 = jnp.sum(terms[:, 1, :], axis=0, keepdims=True)
    used = lanes((1, LN)) < members
    m0 = jnp.where(used, m0, 1.0)
    m1 = jnp.where(used, m1, 1.0)
    mean = m1 / m0
    off = mean - terms[:, 2, :]
    vv = terms[:, 3, :] - 2.0 * off * terms[:, 6, :] + off * off * terms[:, 0, :]
    zu = terms[:, 4, :] - off * terms[:, 5, :] + off * off * terms[:, 1, :]
    cross = terms[:, 5, :] - 2.0 * off * terms[:, 1, :]
    vv, zu, cross = (jnp.sum(x, axis=0, keepdims=True) for x in (vv, zu, cross))
    alpha = m0 / m1
    rr = alpha * alpha * vv
    beta = rr / m0
    alpha_next = rr / (alpha * alpha * zu - alpha * beta * cross + beta * beta * m1)
    one = alpha + alpha_next * (1.0 + beta)
    two = alpha * alpha_next
    table = jnp.concatenate([one, two, jnp.zeros((LN - 2, LN), F32)], axis=0).T
    one, two = table[:members, 0:1], table[:members, 1:2]

    copies = []
    lane = lanes((2 * members, LN))
    for b in range(blocks):
        offset = ints[b]
        number = ints[b + 1] - offset
        base = (offset // LN) * LN
        shift = offset - base
        back = lax.rem(LN - shift, LN)
        keep = lane < LN - shift
        turned = []
        for k in range(3):
            where = at(base + k * LN, LN)
            r, y, yy = vec[:, where], image[:, where], second[:, where]
            both = jnp.concatenate([one * r - two * y, r - one * y + two * yy], axis=0)
            turned.append(pltpu.roll(both, back, 1))
        for k in range(2):
            part = jnp.where(keep, turned[k], turned[k + 1])
            part = jnp.where(lane + k * LN < number, part, 0.0)
            solution_ref[b, :, k * LN : (k + 1) * LN] = part[:members]
            residual_ref[b, :, k * LN : (k + 1) * LN] = part[members:]
        for k, (src, dst) in enumerate(((solution_ref, solution_out), (residual_ref, residual_out))):
            copy = pltpu.make_async_copy(src.at[b], dst.at[b], sems.at[k, b])
            copy.start()
            copies.append(copy)
    for copy in copies:
        copy.wait()


def exchange(first, second):
    devices = lax.axis_size("region")
    received = []
    for start, block in ((1, first), (0, second)):
        pairs = [(i, i + 1) for i in range(start, devices - 1, 2)]
        received.append(lax.ppermute(block, "region", pairs + [(b, a) for a, b in pairs]))
    return received


def call(kernel, name, in_specs, outs, scratch=(), limit=9 * MB, cost=None):
    return pl.pallas_call(
        kernel,
        name=name,
        in_specs=in_specs,
        out_specs=[spec for spec, _ in outs],
        out_shape=[shape for _, shape in outs],
        scratch_shapes=list(scratch),
        compiler_params=pltpu.CompilerParams(vmem_limit_bytes=limit),
        cost_estimate=cost,
    )


def body(obs_pos, obs_sigma, obs_error, innovation, obs_count, pair_list, pair_live):
    blocks, members, _ = innovation.shape
    sd = jax.ShapeDtypeStruct
    in_hbm = functools.partial(pltpu.with_memory_space_constraint, memory_space=pltpu.HBM)
    in_vmem = functools.partial(pltpu.with_memory_space_constraint, memory_space=pltpu.VMEM)
    wide = blocks * CH + 2 * CH
    side_chunks = REACH + 2
    own_slots = [blocks // 2 + 1] * 2 + [OWN_HELD // 2 + 1] * 2
    side_slots = SIDE_HELD // 2 + 1
    listed = blocks * SPAN + 16
    pack_out = (VM, sd((REACH, members + 8, CH), F32))
    again_scratch = [
        pltpu.VMEM((1, CH, LN), F32),
        pltpu.VMEM((1, CH, LN), F32),
        pltpu.VMEM((1, 2 * CH, CH), BF16),
        pltpu.VMEM((1, 2 * CH, CH), BF16),
    ]
    dense = (VM, sd((members, wide), F32))
    tile = (2 * CH, CH)
    column = (VM, sd((blocks, CH, LN), F32))
    *sides, vec, geo, parts, col_x, col_y, ints, floats, down, across = call(
        prepare_kernel, "prepare", [HB] * 5,
        [
            pack_out,
            pack_out,
            dense,
            (VM, sd((8, wide), F32)),
            (VM, sd((blocks, 2 * members, CH), BF16)),
            column,
            column,
            (SM, sd((blocks + 2,), I32)),
            (SM, sd((2 * blocks + 1,), F32)),
            (SM, sd((listed,), I32)),
            (SM, sd((listed,), I32)),
        ],
        [
            pltpu.VMEM(innovation.shape, F32),
            pltpu.VMEM(obs_pos.shape, F32),
            pltpu.VMEM(obs_sigma.shape, F32),
            pltpu.VMEM(obs_error.shape, F32),
            pltpu.SMEM(obs_count.shape, I32),
            pltpu.SemaphoreType.DMA((7,)),
        ],
        limit=9 * MB,
    )(*map(in_hbm, (innovation, obs_pos, obs_sigma, obs_error, obs_count)))
    sides = exchange(*sides)
    *tiles, acc = call(
        own_kernel, "own", [VM, VM, VM, VM, SM, SM, SM],
        [(VM, pltpu.VMEM((slots,) + tile, BF16)) for slots in own_slots] + [dense],
        limit=6 * MB,
        cost=pl.CostEstimate(flops=4 * 10**9, bytes_accessed=20 * MB, transcendentals=0),
    )(geo, parts, col_x, col_y, ints, down, across)
    tiles = map(in_vmem, tiles)
    side = (VM, sd((members, REACH * CH), F32))
    (side_ev, side_od, side_geo, side_ints, side_down, side_across, image, parts,
     *image_sides) = call(
        edge_kernel, "edge", [VM, VM, VM, VM, VM, SM, SM],
        [
            (VM, pltpu.VMEM((side_slots,) + tile, BF16)),
            (VM, pltpu.VMEM((side_slots,) + tile, BF16)),
            (VM, sd((8, 2 * side_chunks * CH), F32)),
            (SM, sd((3,), I32)),
            (SM, sd((128,), I32)),
            (SM, sd((128,), I32)),
            dense,
            (VM, sd((blocks, 2 * members, CH), BF16)),
            side,
            side,
        ],
        [
            pltpu.VMEM((members, 2 * side_chunks * CH), F32),
            pltpu.VMEM((2 * side_chunks, 2 * members, CH), BF16),
            pltpu.VMEM((2 * side_chunks, CH, LN), F32),
            pltpu.VMEM((2 * side_chunks, CH, LN), F32),
            pltpu.SMEM((4 * side_chunks,), F32),
        ],
        limit=7 * MB,
    )(*sides, vec, geo, acc, ints, floats)
    side_ev, side_od = in_vmem(side_ev), in_vmem(side_od)
    image_sides = exchange(*image_sides)
    acc, known = call(
        again_kernel, "again", [VM] * 8 + [SM] * 3,
        [dense, (VM, sd((members, LN), F32))], again_scratch, limit=3 * MB,
        cost=pl.CostEstimate(flops=4 * 10**9, bytes_accessed=20 * MB, transcendentals=0),
    )(*tiles, parts, geo, vec, image, ints, down, across)
    devices = lax.axis_size("region")
    second, sums = call(
        last_kernel, "last", [VM, VM, VM, SM, VM, VM, SM, SM, VM, VM, VM, VM, VM, SM],
        [dense, (VM, sd((devices, 8, LN), F32))],
        [
            pltpu.VMEM((2 * side_chunks, 2 * members, CH), BF16),
            pltpu.VMEM((members, wide), F32),
            *again_scratch,
        ],
        limit=5 * MB,
    )(*image_sides, side_geo, side_ints, side_ev, side_od, side_down, side_across,
      acc, known, vec, image, geo, ints)
    sums = lax.all_to_all(sums, "region", 0, 0)
    field = (HB, sd((blocks, members, CH), F32))
    return tuple(call(
        update_kernel, "update", [VM, VM, VM, VM, SM], [field, field],
        [
            pltpu.VMEM((blocks, members, CH), F32),
            pltpu.VMEM((blocks, members, CH), F32),
            pltpu.SemaphoreType.DMA((2, blocks)),
        ],
        limit=6 * MB,
    )(sums, vec, image, second, ints))


def solution(mesh):
    return jax.shard_map(
        body,
        mesh=mesh,
        in_specs=(
            P(("groups", "region"), None, None),
            P(("groups", "region"), None),
            P(("groups", "region"), None),
            P(("groups", "region"), None, None),
            P(("groups", "region")),
            P(None, ("groups", "region")),
            P(("groups", "region")),
        ),
        out_specs=(P(("groups", "region"), None, None), P(("groups", "region"), None, None)),
        check_vma=False,
    )
```
